256 devices in a mesh: replica: 32 (over y, x, core), tensor: 8 (over z).
Axes of the slice: x: 4, y: 4, z: 8, core: 2. Of those that a mesh axis runs over, the one named last changes fastest.
Arguments:
- normed_token_input: bfloat16 [8192, 2, 8192], P('replica', None, 'tensor'), may hold values from -6 to 6
- rotated_base_query: bfloat16 [8192, 2, 8192], P('replica', None, 'tensor')
- key_value_weight: bfloat16 [8192, 2, 1024], P(None, None, 'tensor'), may hold values from -0.0625 to 0.0625
- key_value_cache: bfloat16 [8192, 2, 32, 1024], P('replica', None, None, 'tensor')
- adapter_down_maps: bfloat16 [128, 192, 8192], P('replica', None, 'tensor'), may hold values from -0.0625 to 0.0625
- query_up_maps: bfloat16 [128, 64, 8192], P('replica', None, 'tensor'), may hold values from -0.75 to 0.75
- key_value_up_maps: bfloat16 [128, 2, 64, 1024], P('replica', None, None, 'tensor'), may hold values from -0.75 to 0.75
- adapter_storage_row: int32 [128], replicated, may hold values from 0 to 127, as said below
- segment_adapter: int32 [512], replicated, may hold values from 0 to 127, as said below
- segment_live_requests: int32 [512], P('replica'), may hold values from 1 to 16, as said below
- cache_length: int32 [8192], P('replica'), may hold values from 2 to 32
Outputs:
- attention: bfloat16 [8192, 2, 8192], P('replica', None, 'tensor')
The draws below stay inside these ranges and needn't reach their ends.
Inputs may be any that keep to these rules, and one draw needn't show every extreme that they name: Adapter a is stored at row adapter_storage_row[a] of adapter_down_maps, query_up_maps and key_value_up_maps; every row once; rows k * 4 to (k + 1) * 4 - 1 form owner group k. `segment_adapter`: segments s * 16 to (s + 1) * 16 - 1 belong to replica s; the segments of one replica use adapters of different owner groups. The first segment_live_requests[s] request slots of segment s are live, the rest are padding.
All inputs are finite; a program needn't handle non-finite values.
Results may differ from the reference program's by a relative error of at most 0.0066.
Values may be sent and summed in bfloat16 or wider, within the bound.
A program may use at most 192 MiB of HBM per device.

```python
import math
import jax
import jax.numpy as jnp
from jax import lax

MODEL_WIDTH = 8192
QUERY_HEAD_COUNT = 64
KV = 8
HEAD_WIDTH = 128
ADAPTER_RANK = 64
SEG_REQ = 16
ADP_REP = 4
CTX = 32
SEGS = 16
REQUEST_SLOTS = 8192
SEG_ALL = 512
ADAPTER_COUNT = 128
N_REPLICA = 32


def route_tables(key):
    popular = jax.random.permutation(jax.random.fold_in(key, 101), N_REPLICA)
    hot_count = max(N_REPLICA // 8, 1)
    boost = jnp.where(popular < hot_count, 4, 1).astype(jnp.int32)
    scores = jax.random.randint(jax.random.fold_in(key, 102), (N_REPLICA, N_REPLICA), 0, 4096) * boost[None, :]
    scores = scores * N_REPLICA + jnp.arange(N_REPLICA, dtype=jnp.int32)[None, :]
    top_values, groups = lax.top_k(scores, SEGS)
    local = jax.random.randint(jax.random.fold_in(key, 103), (N_REPLICA, SEGS), 0, ADP_REP)
    slots = (groups.astype(jnp.int32) * ADP_REP + local).reshape(-1)
    placement = jax.random.permutation(jax.random.fold_in(key, 104), ADAPTER_COUNT).astype(jnp.int32)
    inverse = jnp.argsort(placement, stable=True).astype(jnp.int32)
    return (placement, inverse[slots])


def cache_field(key):
    base = jax.random.normal(jax.random.fold_in(key, 201), (REQUEST_SLOTS, 2, CTX, KV * HEAD_WIDTH), jnp.float32)
    second = base[:, 0, 1]
    return base.at[:, 0, 1].set(second)


def draw_adapter_storage_row(key, part):
    placement, chosen = route_tables(key)
    return placement


def draw_segment_adapter(key, part):
    placement, chosen = route_tables(key)
    return chosen


def draw_segment_live_requests(key, part):
    key = jax.random.fold_in(key, 5)
    counts = jax.random.randint(jax.random.fold_in(key, 1), (SEG_ALL,), 1, SEG_REQ + 1)
    target = jax.random.randint(jax.random.fold_in(key, 2), (), 0, SEG_ALL)
    return counts.at[target].set(SEG_REQ).astype(jnp.int32)


def draw_cache_length(key, part):
    key = jax.random.fold_in(key, 6)
    lengths = jax.random.randint(jax.random.fold_in(key, 1), (REQUEST_SLOTS,), 2, CTX + 1)
    target = jax.random.randint(jax.random.fold_in(key, 2), (), 0, REQUEST_SLOTS)
    return lengths.at[target].set(CTX).astype(jnp.int32)


def draw_key_value_cache(key, part):
    values = cache_field(key)
    return values.astype(jnp.bfloat16)


def draw_rotated_base_query(key, part):
    key = jax.random.fold_in(key, 7)
    values = jax.random.normal(jax.random.fold_in(key, 1), (REQUEST_SLOTS, 2, QUERY_HEAD_COUNT * HEAD_WIDTH), jnp.float32)
    return values.astype(jnp.bfloat16)


def block_levels(own_key, dims, shards, low, largest):
    def one(position, shards_of):
        draws = jax.random.uniform(jax.random.fold_in(jax.random.fold_in(own_key, 6), position), (shards_of,), jnp.float32, low / len(shards), largest / len(shards))
        return jnp.repeat(jnp.exp(draws), dims[position] // shards_of).reshape((-1,) + (1,) * (len(dims) - position - 1))

    gain = one(*shards[0])
    for cut in shards[1:]:
        gain = gain * one(*cut)
    return gain


def centred(key, dims, scale, reach, pieces=(), kind=jnp.bfloat16):
    result = jax.random.normal(key, dims, jnp.float32) * scale
    if len(pieces) > 0:
        result = block_levels(key, dims, pieces, -0.22, 0.18) * result
    return jnp.clip(result, min=-reach, max=reach).astype(kind)


def setup_inputs(seed: int = 0) -> dict:
    seeds = jax.random.split(jax.random.key(seed), 12)
    normed_token_input = centred(seeds[0], (REQUEST_SLOTS, 2, MODEL_WIDTH), 1.0, 6.0, ((0, 32), (2, 8)))
    rotated_base_query = draw_rotated_base_query(jax.random.fold_in(seeds[11], 71), 0)
    key_value_weight = centred(seeds[2], (MODEL_WIDTH, 2, KV * HEAD_WIDTH), MODEL_WIDTH ** -0.5, 0.0625, ((2, 8),))
    key_value_cache = draw_key_value_cache(jax.random.fold_in(seeds[11], 71), 0)
    adapter_down_maps = centred(seeds[4], (ADAPTER_COUNT, 3 * ADAPTER_RANK, MODEL_WIDTH), MODEL_WIDTH ** -0.5, 0.0625, ((0, 32), (2, 8)))
    query_up_maps = centred(seeds[5], (ADAPTER_COUNT, ADAPTER_RANK, QUERY_HEAD_COUNT * HEAD_WIDTH), ADAPTER_RANK ** -0.5, 0.75, ((0, 32), (2, 8)))
    key_value_up_maps = centred(seeds[6], (ADAPTER_COUNT, 2, ADAPTER_RANK, KV * HEAD_WIDTH), ADAPTER_RANK ** -0.5, 0.75, ((0, 32), (3, 8)))
    adapter_storage_row = draw_adapter_storage_row(jax.random.fold_in(seeds[11], 71), 0)
    segment_adapter = draw_segment_adapter(jax.random.fold_in(seeds[11], 71), 0)
    segment_live_requests = draw_segment_live_requests(jax.random.fold_in(seeds[11], 71), 0)
    cache_length = draw_cache_length(jax.random.fold_in(seeds[11], 71), 0)
    return dict(normed_token_input=normed_token_input, rotated_base_query=rotated_base_query, key_value_weight=key_value_weight, key_value_cache=key_value_cache, adapter_down_maps=adapter_down_maps, query_up_maps=query_up_maps, key_value_up_maps=key_value_up_maps, adapter_storage_row=adapter_storage_row, segment_adapter=segment_adapter, segment_live_requests=segment_live_requests, cache_length=cache_length)


ADAPTER_SCALE = 0.5

def reference(normed_token_input, rotated_base_query, key_value_weight, key_value_cache, adapter_down_maps, query_up_maps, key_value_up_maps, adapter_storage_row, segment_adapter, segment_live_requests, cache_length):
    head_column_span = KV * HEAD_WIDTH
    flat_rows = normed_token_input.reshape(REQUEST_SLOTS * 2, MODEL_WIDTH)
    base_kv = jnp.dot(flat_rows, key_value_weight.reshape(MODEL_WIDTH, 2 * head_column_span), preferred_element_type=jnp.float32)
    base_quartet = base_kv.reshape(REQUEST_SLOTS, 2, 2, head_column_span)
    seg_slots = adapter_storage_row[segment_adapter].astype(jnp.int32)
    seg_inputs = normed_token_input.reshape(SEG_ALL, SEG_REQ * 2, MODEL_WIDTH)

    def one_segment(operands):
        inputs, storage_slot_index = operands
        down_weight_matrix = lax.dynamic_index_in_dim(adapter_down_maps, storage_slot_index, 0, keepdims=False)
        up_query = lax.dynamic_index_in_dim(query_up_maps, storage_slot_index, 0, keepdims=False)
        up_pair = lax.dynamic_index_in_dim(key_value_up_maps, storage_slot_index, 0, keepdims=False)
        shrink = jnp.dot(inputs, down_weight_matrix.T, preferred_element_type=jnp.float32).astype(jnp.bfloat16)
        query_correction = jnp.dot(shrink[:, :ADAPTER_RANK], up_query, preferred_element_type=jnp.float32).astype(jnp.bfloat16)
        key_correction = jnp.dot(shrink[:, ADAPTER_RANK:2 * ADAPTER_RANK], up_pair[0], preferred_element_type=jnp.float32).astype(jnp.bfloat16)
        value_correction = jnp.dot(shrink[:, 2 * ADAPTER_RANK:], up_pair[1], preferred_element_type=jnp.float32).astype(jnp.bfloat16)
        return (query_correction, key_correction, value_correction)
    query_correction, key_correction, value_correction = lax.map(one_segment, (seg_inputs, seg_slots))
    query_rows = (rotated_base_query.astype(jnp.float32) + ADAPTER_SCALE * query_correction.reshape(REQUEST_SLOTS, 2, QUERY_HEAD_COUNT * HEAD_WIDTH).astype(jnp.float32)).astype(jnp.bfloat16)
    incoming_keys = (base_quartet[:, :, 0] + ADAPTER_SCALE * key_correction.reshape(REQUEST_SLOTS, 2, head_column_span).astype(jnp.float32)).astype(jnp.bfloat16)
    incoming_values = (base_quartet[:, :, 1] + ADAPTER_SCALE * value_correction.reshape(REQUEST_SLOTS, 2, head_column_span).astype(jnp.float32)).astype(jnp.bfloat16)
    group_size = QUERY_HEAD_COUNT // KV
    inv_root = 1.0 / math.sqrt(HEAD_WIDTH)
    per_block = REQUEST_SLOTS // N_REPLICA

    def attend(block):
        query_block, cache_block, key_block, value_block, length_block = block
        query_heads = query_block.reshape(per_block, 2, KV, group_size, HEAD_WIDTH).astype(jnp.float32)
        cache_keys = cache_block[:, 0].reshape(per_block, CTX, KV, HEAD_WIDTH).astype(jnp.float32)
        cache_values = cache_block[:, 1].reshape(per_block, CTX, KV, HEAD_WIDTH).astype(jnp.float32)
        keys_all = jnp.concatenate([cache_keys, key_block.reshape(per_block, 2, KV, HEAD_WIDTH).astype(jnp.float32)], axis=1)
        values_all = jnp.concatenate([cache_values, value_block.reshape(per_block, 2, KV, HEAD_WIDTH).astype(jnp.float32)], axis=1)
        scores = jnp.einsum('rpkgd,rjkd->rkgpj', query_heads, keys_all) * inv_root
        key_spots = jnp.arange(CTX + 2, dtype=jnp.int32)
        cached_ok = key_spots[None, :] < length_block[:, None]
        fresh_ok = key_spots[None, :] - CTX <= jnp.arange(2, dtype=jnp.int32)[:, None]
        allowed = jnp.where(key_spots[None, None, :] >= CTX, fresh_ok[None], cached_ok[:, None, :])
        scores = jnp.where(allowed[:, None, None], scores, -jnp.inf)
        row_top = lax.optimization_barrier(jnp.max(scores, axis=4, keepdims=True))
        lifted = jnp.exp(scores - row_top)
        weights = (lifted / lax.optimization_barrier(jnp.sum(lifted, axis=4, keepdims=True))).astype(jnp.bfloat16)
        return jnp.einsum('rkgpj,rjkd->rpkgd', weights.astype(jnp.float32), values_all)
    blocks = (query_rows.reshape(N_REPLICA, per_block, 2, QUERY_HEAD_COUNT * HEAD_WIDTH), key_value_cache.reshape(N_REPLICA, per_block, 2, CTX, head_column_span), incoming_keys.reshape(N_REPLICA, per_block, 2, head_column_span), incoming_values.reshape(N_REPLICA, per_block, 2, head_column_span), cache_length.reshape(N_REPLICA, per_block))
    attended = lax.map(attend, blocks).reshape(REQUEST_SLOTS, 2, KV, group_size, HEAD_WIDTH)
    seg_slot = jnp.arange(REQUEST_SLOTS, dtype=jnp.int32) % SEG_REQ
    live_rows = seg_slot < jnp.repeat(segment_live_requests, SEG_REQ)
    attended = jnp.where(live_rows[:, None, None, None, None], attended, 0.0)
    return attended.reshape(REQUEST_SLOTS, 2, QUERY_HEAD_COUNT * HEAD_WIDTH).astype(jnp.bfloat16)
```

```python
import functools
import math

import jax
import jax.numpy as jnp
from jax import lax
from jax.experimental import pallas as pl
from jax.experimental.pallas import tpu as pltpu
from jax.sharding import PartitionSpec as P

HEAD_WIDTH = 128
CTX = 32
ADAPTER_SCALE = 0.5
MESH = pl.DeviceIdType.MESH

RINGS = (
    ((2, 2),),
    ((2, 1), (1, 2), (2, 3), (3, 2)),
    ((0, 2), (2, 0)),
    ((1, 1), (3, 3), (1, 3), (3, 1)),
    ((0, 1), (1, 0), (0, 3), (3, 0)),
)
OFFSETS = [(0, 0, 0)] + [(dy, dx, dc) for ring in RINGS for dc in (0, 1) for dy, dx in ring] + [(0, 0, 1)]
SLOTS = 32
CHUNKS = 4
PER = SLOTS // CHUNKS
TZ = 8


def packed(chunk, which, bits):
    total = 0
    for j in range(PER):
        total += OFFSETS[chunk * PER + j][which] << (bits * j)
    return total


PACK_Y = [packed(c, 0, 2) for c in range(CHUNKS)]
PACK_X = [packed(c, 1, 2) for c in range(CHUNKS)]
PACK_C = [packed(c, 2, 1) for c in range(CHUNKS)]


def offset(chunk, j):
    return (
        (PACK_Y[chunk] >> (2 * j)) & 3,
        (PACK_X[chunk] >> (2 * j)) & 3,
        (PACK_C[chunk] >> j) & 1,
    )


def moved(me, off, sign):
    y, x, c = me // 8, (me // 2) % 4, me % 2
    dy, dx, dc = off
    return ((y + 4 + sign * dy) % 4) * 8 + ((x + 4 + sign * dx) % 4) * 2 + (c + dc) % 2


def exchange_kernel(
    seg_of_group, group_of_seg, local_of_replica, x_ref, down_ref, upq_ref, upkv_ref, out_ref,
    xs, xr, part, rs, ag, ds, dr,
    x_send, x_recv, rs_send, rs_recv, ag_send, ag_recv, d_send, d_recv,
):
    me = lax.axis_index("replica")
    t = lax.axis_index("tensor")

    barrier = pltpu.get_barrier_semaphore()

    def greet_plane(i, _):
        pl.semaphore_signal(barrier, inc=1, device_id=((me + i) % SLOTS, t), device_id_type=MESH)
        return 0

    def greet_z(i, _):
        pl.semaphore_signal(barrier, inc=1, device_id=(me, (t + i) % TZ), device_id_type=MESH)
        return 0

    lax.fori_loop(1, SLOTS, greet_plane, 0)
    lax.fori_loop(1, TZ, greet_z, 0)

    def x_copy(chunk, j):
        p = chunk * PER + j
        return pltpu.make_async_remote_copy(
            src_ref=xs.at[p], dst_ref=xr.at[p], send_sem=x_send.at[p], recv_sem=x_recv.at[p],
            device_id=(moved(me, offset(chunk, j), 1), t), device_id_type=MESH,
        )

    def d_copy(chunk, j):
        p = chunk * PER + j
        return pltpu.make_async_remote_copy(
            src_ref=ds.at[p], dst_ref=dr.at[me], send_sem=d_send.at[p], recv_sem=d_recv.at[p],
            device_id=(moved(me, offset(chunk, j), -1), t), device_id_type=MESH,
        )

    def rs_copy(chunk, u, sender):
        return pltpu.make_async_remote_copy(
            src_ref=part.at[chunk * PER + u], dst_ref=rs.at[chunk, sender],
            send_sem=rs_send.at[chunk, u], recv_sem=rs_recv.at[chunk, sender],
            device_id=(me, u), device_id_type=MESH,
        )

    def ag_copy(chunk, u, sender):
        return pltpu.make_async_remote_copy(
            src_ref=ag.at[chunk, sender], dst_ref=ag.at[chunk, sender],
            send_sem=ag_send.at[chunk, u], recv_sem=ag_recv.at[chunk, sender],
            device_id=(me, u), device_id_type=MESH,
        )

    for chunk in range(CHUNKS):
        def fill(j, _, chunk=chunk):
            group = moved(me, offset(chunk, j), 1)
            xs[chunk * PER + j] = x_ref[seg_of_group[group]]
            return 0

        lax.fori_loop(0, PER, fill, 0)
    pl.semaphore_wait(barrier, SLOTS - 1 + TZ - 1)
    for chunk in range(CHUNKS):
        def send(j, _, chunk=chunk):
            x_copy(chunk, j).start()
            return 0

        lax.fori_loop(1 if chunk == 0 else 0, PER, send, 0)

    def shrink_parts(chunk):
        def one(j, _):
            p = chunk * PER + j
            rows = xs[0] if chunk == 0 and isinstance(j, int) else xr[p]
            w = down_ref[local_of_replica[moved(me, offset(chunk, j), -1)]]
            part[p] = lax.dot_general(
                rows, w, (((1,), (1,)), ((), ())), preferred_element_type=jnp.float32
            ).astype(jnp.bfloat16)
            return 0

        def arrived(j, _):
            x_copy(chunk, j).wait_recv()
            return one(j, 0)

        if chunk == 0:
            one(0, 0)
        lax.fori_loop(1 if chunk == 0 else 0, PER, arrived, 0)

        def send(i, _):
            rs_copy(chunk, (t + i) % TZ, t).start()
            return 0

        lax.fori_loop(1, TZ, send, 0)

    def add_up(chunk):
        def wait(i, _):
            rs_copy(chunk, t, (t + TZ - i) % TZ).wait_recv()
            return 0

        lax.fori_loop(1, TZ, wait, 0)
        rs[chunk, t] = part[chunk * PER + t]
        total = rs[chunk, 0].astype(jnp.float32)
        for u in range(1, TZ):
            total = total + rs[chunk, u].astype(jnp.float32)
        ag[chunk, t] = total.astype(jnp.bfloat16)

        def send(i, _):
            ag_copy(chunk, (t + i) % TZ, t).start()
            return 0

        lax.fori_loop(1, TZ, send, 0)

    def give_back(chunk):
        def wait(i, _):
            ag_copy(chunk, t, (t + TZ - i) % TZ).wait_recv()
            return 0

        lax.fori_loop(1, TZ, wait, 0)

        def deltas(j):
            a = local_of_replica[moved(me, offset(chunk, j), -1)]
            shrink = ag[chunk, j]
            q = jnp.dot(shrink[:, 0:64], upq_ref[a], preferred_element_type=jnp.float32)
            k = jnp.dot(shrink[:, 64:128], upkv_ref[a, 0], preferred_element_type=jnp.float32)
            v = jnp.dot(shrink[:, 128:192], upkv_ref[a, 1], preferred_element_type=jnp.float32)
            return jnp.concatenate([q, k, v], axis=1).astype(jnp.bfloat16)

        def one(j, _):
            ds[chunk * PER + j] = deltas(j)
            d_copy(chunk, j).start()
            return 0

        if chunk == 0:
            dr[me] = deltas(0)
        lax.fori_loop(1 if chunk == 0 else 0, PER, one, 0)

    shrink_parts(0)
    shrink_parts(1)
    add_up(0)
    shrink_parts(2)
    add_up(1)
    give_back(0)
    shrink_parts(3)
    add_up(2)
    give_back(1)
    add_up(3)
    give_back(2)
    give_back(3)

    for chunk in range(CHUNKS):
        def settle(j, _, chunk=chunk):
            d_copy(chunk, j).wait_recv()
            return 0

        lax.fori_loop(1 if chunk == 0 else 0, PER, settle, 0)

    def gather(s, _):
        out_ref[s] = dr[group_of_seg[s]]
        return 0

    lax.fori_loop(0, out_ref.shape[0], gather, 0)

    for chunk in range(CHUNKS):
        def settle(j, _, chunk=chunk):
            x_copy(chunk, j).wait_send()
            d_copy(chunk, j).wait_send()
            return 0

        lax.fori_loop(1 if chunk == 0 else 0, PER, settle, 0)

        def settle_z(i, _, chunk=chunk):
            rs_copy(chunk, (t + i) % TZ, t).wait_send()
            ag_copy(chunk, (t + i) % TZ, t).wait_send()
            return 0

        lax.fori_loop(1, TZ, settle_z, 0)


def exchange(seg_of_group, group_of_seg, local_of_replica, x, down, upq, upkv):
    segs, rows, features = x.shape
    ranks = down.shape[1]
    columns = upq.shape[2] + 2 * upkv.shape[3]
    smem = pl.BlockSpec(memory_space=pltpu.SMEM)
    vmem = pl.BlockSpec(memory_space=pltpu.VMEM)
    dma = pltpu.SemaphoreType.DMA
    return pl.pallas_call(
        exchange_kernel,
        out_shape=jax.ShapeDtypeStruct((segs, rows, columns), jnp.bfloat16),
        in_specs=[smem] * 3 + [vmem] * 4,
        out_specs=vmem,
        scratch_shapes=[
            pltpu.VMEM((SLOTS, rows, features), jnp.bfloat16),
            pltpu.VMEM((SLOTS, rows, features), jnp.bfloat16),
            pltpu.VMEM((SLOTS, rows, ranks), jnp.bfloat16),
            pltpu.VMEM((CHUNKS, TZ, rows, ranks), jnp.bfloat16),
            pltpu.VMEM((CHUNKS, TZ, rows, ranks), jnp.bfloat16),
            pltpu.VMEM((SLOTS, rows, columns), jnp.bfloat16),
            pltpu.VMEM((SLOTS, rows, columns), jnp.bfloat16),
            dma((SLOTS,)), dma((SLOTS,)),
            dma((CHUNKS, TZ)), dma((CHUNKS, TZ)), dma((CHUNKS, TZ)), dma((CHUNKS, TZ)),
            dma((SLOTS,)), dma((SLOTS,)),
        ],
        compiler_params=pltpu.CompilerParams(
            collective_id=0, has_side_effects=True, vmem_limit_bytes=40 * 2**20
        ),
        cost_estimate=pl.CostEstimate(flops=10**9, bytes_accessed=200 * 2**20, transcendentals=0),
        name="exchange",
    )(seg_of_group, group_of_seg, local_of_replica, x, down, upq, upkv)


def attend_kernel(live, q_ref, delta_ref, base_ref, cache_ref, bias_ref, out_ref):
    s = pl.program_id(0)
    heads = q_ref.shape[1] // HEAD_WIDTH
    wide = q_ref.shape[1]
    half = 8
    delta = delta_ref[0].astype(jnp.float32) * ADAPTER_SCALE
    q_all = (q_ref[...].astype(jnp.float32) + delta[:, :wide]).astype(jnp.bfloat16)
    fresh = (base_ref[...] + delta[:, wide:]).astype(jnp.bfloat16)
    rows = half * 2
    n = heads * rows
    row = lax.broadcasted_iota(jnp.int32, (n, half * CTX), 0)
    col = lax.broadcasted_iota(jnp.int32, (n, half * CTX), 1)
    same = (row % rows) // 2 == col // CTX
    row = lax.broadcasted_iota(jnp.int32, (n, rows), 0) % rows
    col = lax.broadcasted_iota(jnp.int32, (n, rows), 1)
    same_fresh = (row // 2 == col // 2) & (col <= row)
    scale = 1.0 / math.sqrt(HEAD_WIDTH)
    for h in range(2):
        at = slice(h * rows, (h + 1) * rows)
        q = jnp.concatenate(
            [q_all[at, g * HEAD_WIDTH : (g + 1) * HEAD_WIDTH] for g in range(heads)], axis=0
        )
        keys = cache_ref[h * half : (h + 1) * half, 0].reshape(half * CTX, HEAD_WIDTH)
        values = cache_ref[h * half : (h + 1) * half, 1].reshape(half * CTX, HEAD_WIDTH)
        new_keys = fresh[at, :HEAD_WIDTH]
        new_values = fresh[at, HEAD_WIDTH:]
        nt = (((1,), (1,)), ((), ()))
        old = lax.dot_general(q, keys, nt, preferred_element_type=jnp.float32) * scale
        new = lax.dot_general(q, new_keys, nt, preferred_element_type=jnp.float32) * scale
        old = jnp.where(same, old + bias_ref[0, h : h + 1], -jnp.inf)
        new = jnp.where(same_fresh, new, -jnp.inf)
        top = jnp.maximum(
            jnp.max(old, axis=1, keepdims=True), jnp.max(new, axis=1, keepdims=True)
        )
        old = jnp.exp(old - top)
        new = jnp.exp(new - top)
        total = jnp.sum(old, axis=1, keepdims=True) + jnp.sum(new, axis=1, keepdims=True)
        mixed = jnp.dot(old.astype(jnp.bfloat16), values, preferred_element_type=jnp.float32)
        mixed = mixed + jnp.dot(
            new.astype(jnp.bfloat16), new_values, preferred_element_type=jnp.float32
        )
        mixed = mixed / total
        out = jnp.concatenate([mixed[g * rows : (g + 1) * rows] for g in range(heads)], axis=1)
        place = h * half + lax.broadcasted_iota(jnp.int32, out.shape, 0) // 2
        out_ref[at, :] = jnp.where(place < live[s], out, 0.0).astype(jnp.bfloat16)


def attend(live, q, delta, base, cache, bias):
    segs = live.shape[0]
    rows, wide = q.shape
    per = rows // segs
    return pl.pallas_call(
        attend_kernel,
        grid_spec=pltpu.PrefetchScalarGridSpec(
            num_scalar_prefetch=1,
            grid=(segs,),
            in_specs=[
                pl.BlockSpec((per, wide), lambda s, _: (s, 0)),
                pl.BlockSpec((1,) + delta.shape[1:], lambda s, _: (s, 0, 0)),
                pl.BlockSpec((per, base.shape[1]), lambda s, _: (s, 0)),
                pl.BlockSpec((cache.shape[0] // segs,) + cache.shape[1:], lambda s, _: (s, 0, 0, 0)),
                pl.BlockSpec((1,) + bias.shape[1:], lambda s, _: (s, 0, 0)),
            ],
            out_specs=pl.BlockSpec((per, wide), lambda s, _: (s, 0)),
        ),
        out_shape=jax.ShapeDtypeStruct((rows, wide), jnp.bfloat16),
        compiler_params=pltpu.CompilerParams(vmem_limit_bytes=24 * 2**20),
        name="attend",
    )(live, q, delta, base, cache, bias)


def shards(
    normed_token_input,
    rotated_base_query,
    key_value_weight,
    key_value_cache,
    adapter_down_maps,
    query_up_maps,
    key_value_up_maps,
    adapter_storage_row,
    segment_adapter,
    segment_live_requests,
    cache_length,
):
    requests, tokens, features = normed_token_input.shape
    wide = rotated_base_query.shape[2]
    kv_wide = key_value_weight.shape[2]
    owned = adapter_down_maps.shape[0]
    replicas = lax.axis_size("replica")
    segs = segment_live_requests.shape[0]
    me = lax.axis_index("replica")

    adapter_ids = jnp.arange(adapter_storage_row.shape[0], dtype=jnp.int32)
    slot = jnp.sum(
        jnp.where(
            segment_adapter[:, None] == adapter_ids[None, :], adapter_storage_row[None, :], 0
        ),
        axis=1,
    ).reshape(replicas, segs)
    group, local = slot // owned, slot % owned
    group_of_seg = lax.dynamic_index_in_dim(group, me, 0, keepdims=False)
    group_ids = jnp.arange(replicas, dtype=jnp.int32)
    seg_ids = jnp.arange(segs, dtype=jnp.int32)
    seg_of_group = jnp.sum(
        jnp.where(group_of_seg[None, :] == group_ids[:, None], seg_ids[None, :], 0), axis=1
    )
    local_of_replica = jnp.sum(jnp.where(group == me, local, 0), axis=1)

    gathered = lax.all_gather(normed_token_input, "tensor", axis=2, tiled=True)
    base_kv = jnp.dot(
        gathered.reshape(-1, gathered.shape[2]),
        key_value_weight.reshape(-1, 2 * kv_wide),
        preferred_element_type=jnp.float32,
    )
    delta = exchange(
        seg_of_group, group_of_seg, local_of_replica,
        normed_token_input.reshape(segs, requests * tokens // segs, features),
        adapter_down_maps, query_up_maps, key_value_up_maps,
    )
    spots = jnp.arange(CTX, dtype=jnp.int32)
    bias = jnp.where(spots[None, :] < cache_length[:, None], 0.0, -jnp.inf).astype(jnp.float32)
    out = attend(
        segment_live_requests, rotated_base_query.reshape(requests * tokens, wide), delta, base_kv,
        key_value_cache, bias.reshape(segs, 2, requests // segs // 2 * CTX),
    )
    return out.reshape(requests, tokens, wide)


def solution(mesh):
    return jax.shard_map(
        shards,
        mesh=mesh,
        in_specs=(
            P("replica", None, "tensor"),
            P("replica", None, "tensor"),
            P(None, None, "tensor"),
            P("replica", None, None, "tensor"),
            P("replica", None, "tensor"),
            P("replica", None, "tensor"),
            P("replica", None, None, "tensor"),
            P(),
            P(),
            P("replica"),
            P("replica"),
        ),
        out_specs=P("replica", None, "tensor"),
        check_vma=False,
    )
```

```python
import functools
import math

import jax
import jax.numpy as jnp
from jax import lax
from jax.experimental import pallas as pl
from jax.experimental.pallas import tpu as pltpu
from jax.sharding import PartitionSpec as P

HEAD_WIDTH = 128
CTX = 32
ADAPTER_SCALE = 0.5
MESH = pl.DeviceIdType.MESH

RINGS = (
    ((2, 2),),
    ((2, 1), (1, 2), (2, 3), (3, 2)),
    ((0, 2), (2, 0)),
    ((1, 1), (3, 3), (1, 3), (3, 1)),
    ((0, 1), (1, 0), (0, 3), (3, 0)),
)
OFFSETS = [(0, 0, 0)] + [(dy, dx, dc) for ring in RINGS for dc in (0, 1) for dy, dx in ring] + [(0, 0, 1)]
SLOTS = 32
CHUNKS = 4
PER = SLOTS // CHUNKS
TZ = 8


def packed(chunk, which, bits):
    total = 0
    for j in range(PER):
        total += OFFSETS[chunk * PER + j][which] << (bits * j)
    return total


PACK_Y = [packed(c, 0, 2) for c in range(CHUNKS)]
PACK_X = [packed(c, 1, 2) for c in range(CHUNKS)]
PACK_C = [packed(c, 2, 1) for c in range(CHUNKS)]


def offset(chunk, j):
    return (
        (PACK_Y[chunk] >> (2 * j)) & 3,
        (PACK_X[chunk] >> (2 * j)) & 3,
        (PACK_C[chunk] >> j) & 1,
    )


def moved(me, off, sign):
    y, x, c = me // 8, (me // 2) % 4, me % 2
    dy, dx, dc = off
    return ((y + 4 + sign * dy) % 4) * 8 + ((x + 4 + sign * dx) % 4) * 2 + (c + dc) % 2


def exchange_kernel(
    seg_of_group, group_of_seg, local_of_replica, x_ref, down_ref, upq_ref, upkv_ref, wpart_ref,
    out_ref, base_ref,
    xs, xr, part, rs, ag, ds, dr, wall, right_out, right_in, left_out, left_in,
    x_send, x_recv, rs_send, rs_recv, ag_send, ag_recv, d_send, d_recv,
    wz_send, wz_recv, w1_send, w1_recv, w2_send, w2_recv, w3_send, w3_recv,
    right_send, right_recv, left_send, left_recv,
):
    me = lax.axis_index("replica")
    t = lax.axis_index("tensor")
    y, x, core = me // 8, (me // 2) % 4, me % 2

    barrier = pltpu.get_barrier_semaphore()

    def greet_plane(i, _):
        pl.semaphore_signal(barrier, inc=1, device_id=((me + i) % SLOTS, t), device_id_type=MESH)
        return 0

    def greet_z(i, _):
        pl.semaphore_signal(barrier, inc=1, device_id=(me, (t + i) % TZ), device_id_type=MESH)
        return 0

    lax.fori_loop(1, SLOTS, greet_plane, 0)
    lax.fori_loop(1, TZ, greet_z, 0)

    def x_copy(chunk, j):
        p = chunk * PER + j
        return pltpu.make_async_remote_copy(
            src_ref=xs.at[p], dst_ref=xr.at[p], send_sem=x_send.at[p], recv_sem=x_recv.at[p],
            device_id=(moved(me, offset(chunk, j), 1), t), device_id_type=MESH,
        )

    def d_copy(chunk, j):
        p = chunk * PER + j
        return pltpu.make_async_remote_copy(
            src_ref=ds.at[p], dst_ref=dr.at[me], send_sem=d_send.at[p], recv_sem=d_recv.at[p],
            device_id=(moved(me, offset(chunk, j), -1), t), device_id_type=MESH,
        )

    def rs_copy(chunk, u, sender):
        return pltpu.make_async_remote_copy(
            src_ref=part.at[chunk * PER + u], dst_ref=rs.at[chunk, sender],
            send_sem=rs_send.at[chunk, u], recv_sem=rs_recv.at[chunk, sender],
            device_id=(me, u), device_id_type=MESH,
        )

    def ag_copy(chunk, u, sender):
        return pltpu.make_async_remote_copy(
            src_ref=ag.at[chunk, sender], dst_ref=ag.at[chunk, sender],
            send_sem=ag_send.at[chunk, u], recv_sem=ag_recv.at[chunk, sender],
            device_id=(me, u), device_id_type=MESH,
        )

    def wz_copy(u, sender):
        half = sender // 4
        i = jnp.where(half == 0, y, x)
        j = jnp.where(half == 0, x, y)
        return pltpu.make_async_remote_copy(
            src_ref=wpart_ref.at[u], dst_ref=wall.at[half, core, i, j, sender % 4],
            send_sem=wz_send.at[u], recv_sem=wz_recv.at[sender],
            device_id=(me, u), device_id_type=MESH,
        )

    def along(axis, d):
        if axis == 0:
            return ((y + d) % 4) * 8 + x * 2 + core
        return y * 8 + ((x + d) % 4) * 2 + core

    def w1_copy(half, d):
        piece = wall.at[0, core, y, x] if half == 0 else wall.at[1, core, x, y]
        return pltpu.make_async_remote_copy(
            src_ref=piece, dst_ref=piece, send_sem=w1_send.at[half, d], recv_sem=w1_recv.at[half, d],
            device_id=(along(1 - half, d), t), device_id_type=MESH,
        )

    def w2_copy(half, d):
        piece = wall.at[0, core, y] if half == 0 else wall.at[1, core, x]
        return pltpu.make_async_remote_copy(
            src_ref=piece, dst_ref=piece, send_sem=w2_send.at[half, d], recv_sem=w2_recv.at[half, d],
            device_id=(along(half, d), t), device_id_type=MESH,
        )

    def w3_copy(half, d):
        line = ((y if half == 0 else x) + 4 - d) % 4
        return pltpu.make_async_remote_copy(
            src_ref=wall.at[half, core, line], dst_ref=wall.at[half, core, line],
            send_sem=w3_send.at[half, d], recv_sem=w3_recv.at[half, d],
            device_id=(y * 8 + x * 2 + 1 - core, t), device_id_type=MESH,
        )

    def weight_z():
        def send(i, _):
            wz_copy((t + i) % TZ, t).start()
            return 0

        lax.fori_loop(1, TZ, send, 0)
        half = t // 4
        i = jnp.where(half == 0, y, x)
        j = jnp.where(half == 0, x, y)
        wall[half, core, i, j, t % 4] = wpart_ref[t]

    def weight_first():
        def wait(i, _):
            wz_copy(t, (t + TZ - i) % TZ).wait_recv()
            return 0

        lax.fori_loop(1, TZ, wait, 0)
        for d in (2, 1, 3):
            for half in range(2):
                w1_copy(half, d).start()

    def weight_second():
        for d in (1, 3, 2):
            for half in range(2):
                w1_copy(half, d).wait_recv()
        for d in (2, 1, 3):
            for half in range(2):
                w2_copy(half, d).start()
        for half in range(2):
            w3_copy(half, 0).start()

    def weight_third():
        for d in (1, 3, 2):
            for half in range(2):
                w2_copy(half, d).wait_recv()
                w3_copy(half, d).start()

    def weight_done():
        for d in (0, 1, 3, 2):
            for half in range(2):
                w3_copy(half, d).wait_recv()

    def right_copy(s):
        return pltpu.make_async_remote_copy(
            src_ref=right_out.at[s], dst_ref=right_in.at[s],
            send_sem=right_send.at[s], recv_sem=right_recv.at[s],
            device_id=(me, (t + 1) % TZ), device_id_type=MESH,
        )

    def left_copy(s):
        return pltpu.make_async_remote_copy(
            src_ref=left_out.at[s], dst_ref=left_in.at[s],
            send_sem=left_send.at[s], recv_sem=left_recv.at[s],
            device_id=(me, (t + TZ - 1) % TZ), device_id_type=MESH,
        )

    tall = 256
    tiles = base_ref.shape[0] // tall
    segs_of_tile = tall // x_ref.shape[1]

    def base_part(share, write):
        def tile(i, _):
            w = wall[share // 4, :, :, :, share % 4].reshape(x_ref.shape[2], base_ref.shape[1])
            rows = x_ref[pl.ds(i * segs_of_tile, segs_of_tile)].reshape(tall, x_ref.shape[2])
            write(pl.ds(i * tall, tall), jnp.dot(rows, w, preferred_element_type=jnp.float32))
            return 0

        lax.fori_loop(0, tiles, tile, 0)

    def ring(s):
        if s < 4:
            def to_right(at, value):
                if s > 0:
                    value = value + right_in[s - 1, at].astype(jnp.float32)
                right_out[s, at] = value.astype(jnp.bfloat16)

            if s > 0:
                right_copy(s - 1).wait_recv()
            base_part((t + 4 - s) % TZ, to_right)
            right_copy(s).start()
        if s < 3:
            def to_left(at, value):
                if s > 0:
                    value = value + left_in[s - 1, at].astype(jnp.float32)
                left_out[s, at] = value.astype(jnp.bfloat16)

            if s > 0:
                left_copy(s - 1).wait_recv()
            base_part((t + TZ - 3 + s) % TZ, to_left)
            left_copy(s).start()

    def ring_end():
        def to_base(at, value):
            base_ref[at] = (
                value + right_in[3, at].astype(jnp.float32) + left_in[2, at].astype(jnp.float32)
            )

        left_copy(2).wait_recv()
        right_copy(3).wait_recv()
        base_part(t, to_base)

    for chunk in range(CHUNKS):
        def fill(j, _, chunk=chunk):
            group = moved(me, offset(chunk, j), 1)
            xs[chunk * PER + j] = x_ref[seg_of_group[group]]
            return 0

        lax.fori_loop(0, PER, fill, 0)
    pl.semaphore_wait(barrier, SLOTS - 1 + TZ - 1)
    weight_z()
    for chunk in range(CHUNKS):
        def send(j, _, chunk=chunk):
            x_copy(chunk, j).start()
            return 0

        lax.fori_loop(1 if chunk == 0 else 0, PER, send, 0)

    def shrink_parts(chunk):
        def one(j, _):
            p = chunk * PER + j
            rows = xs[0] if chunk == 0 and isinstance(j, int) else xr[p]
            w = down_ref[local_of_replica[moved(me, offset(chunk, j), -1)]]
            part[p] = lax.dot_general(
                rows, w, (((1,), (1,)), ((), ())), preferred_element_type=jnp.float32
            ).astype(jnp.bfloat16)
            return 0

        def arrived(j, _):
            x_copy(chunk, j).wait_recv()
            return one(j, 0)

        if chunk == 0:
            one(0, 0)
        lax.fori_loop(1 if chunk == 0 else 0, PER, arrived, 0)

        def send(i, _):
            rs_copy(chunk, (t + i) % TZ, t).start()
            return 0

        lax.fori_loop(1, TZ, send, 0)

    def add_up(chunk):
        def wait(i, _):
            rs_copy(chunk, t, (t + TZ - i) % TZ).wait_recv()
            return 0

        lax.fori_loop(1, TZ, wait, 0)
        rs[chunk, t] = part[chunk * PER + t]
        total = rs[chunk, 0].astype(jnp.float32)
        for u in range(1, TZ):
            total = total + rs[chunk, u].astype(jnp.float32)
        ag[chunk, t] = total.astype(jnp.bfloat16)

        def send(i, _):
            ag_copy(chunk, (t + i) % TZ, t).start()
            return 0

        lax.fori_loop(1, TZ, send, 0)

    def give_back(chunk):
        def wait(i, _):
            ag_copy(chunk, t, (t + TZ - i) % TZ).wait_recv()
            return 0

        lax.fori_loop(1, TZ, wait, 0)

        def deltas(j):
            a = local_of_replica[moved(me, offset(chunk, j), -1)]
            shrink = ag[chunk, j]
            q = jnp.dot(shrink[:, 0:64], upq_ref[a], preferred_element_type=jnp.float32)
            k = jnp.dot(shrink[:, 64:128], upkv_ref[a, 0], preferred_element_type=jnp.float32)
            v = jnp.dot(shrink[:, 128:192], upkv_ref[a, 1], preferred_element_type=jnp.float32)
            return jnp.concatenate([q, k, v], axis=1).astype(jnp.bfloat16)

        def one(j, _):
            ds[chunk * PER + j] = deltas(j)
            d_copy(chunk, j).start()
            return 0

        if chunk == 0:
            dr[me] = deltas(0)
        lax.fori_loop(1 if chunk == 0 else 0, PER, one, 0)

    weight_first()
    shrink_parts(0)
    weight_second()
    shrink_parts(1)
    add_up(0)
    shrink_parts(2)
    add_up(1)
    give_back(0)
    shrink_parts(3)
    add_up(2)
    give_back(1)
    weight_third()
    add_up(3)
    give_back(2)
    weight_done()
    ring(0)
    give_back(3)
    ring(1)
    ring(2)
    ring(3)
    ring_end()

    for chunk in range(CHUNKS):
        def settle(j, _, chunk=chunk):
            d_copy(chunk, j).wait_recv()
            return 0

        lax.fori_loop(1 if chunk == 0 else 0, PER, settle, 0)

    def gather(s, _):
        out_ref[s] = dr[group_of_seg[s]]
        return 0

    lax.fori_loop(0, out_ref.shape[0], gather, 0)

    for chunk in range(CHUNKS):
        def settle(j, _, chunk=chunk):
            x_copy(chunk, j).wait_send()
            d_copy(chunk, j).wait_send()
            return 0

        lax.fori_loop(1 if chunk == 0 else 0, PER, settle, 0)

        def settle_z(i, _, chunk=chunk):
            rs_copy(chunk, (t + i) % TZ, t).wait_send()
            ag_copy(chunk, (t + i) % TZ, t).wait_send()
            return 0

        lax.fori_loop(1, TZ, settle_z, 0)

    def settle_w(i, _):
        wz_copy((t + i) % TZ, t).wait_send()
        return 0

    lax.fori_loop(1, TZ, settle_w, 0)
    for half in range(2):
        for d in range(1, 4):
            w1_copy(half, d).wait_send()
            w2_copy(half, d).wait_send()
        for d in range(4):
            w3_copy(half, d).wait_send()
    for s in range(4):
        right_copy(s).wait_send()
    for s in range(3):
        left_copy(s).wait_send()


def exchange(seg_of_group, group_of_seg, local_of_replica, x, down, upq, upkv, wpart):
    segs, rows, features = x.shape
    ranks = down.shape[1]
    columns = upq.shape[2] + 2 * upkv.shape[3]
    kv = wpart.shape[2]
    smem = pl.BlockSpec(memory_space=pltpu.SMEM)
    vmem = pl.BlockSpec(memory_space=pltpu.VMEM)
    dma = pltpu.SemaphoreType.DMA
    return pl.pallas_call(
        exchange_kernel,
        out_shape=(
            jax.ShapeDtypeStruct((segs, rows, columns), jnp.bfloat16),
            jax.ShapeDtypeStruct((segs * rows, kv), jnp.float32),
        ),
        in_specs=[smem] * 3 + [vmem] * 5,
        out_specs=(vmem, vmem),
        scratch_shapes=[
            pltpu.VMEM((SLOTS, rows, features), jnp.bfloat16),
            pltpu.VMEM((SLOTS, rows, features), jnp.bfloat16),
            pltpu.VMEM((SLOTS, rows, ranks), jnp.bfloat16),
            pltpu.VMEM((CHUNKS, TZ, rows, ranks), jnp.bfloat16),
            pltpu.VMEM((CHUNKS, TZ, rows, ranks), jnp.bfloat16),
            pltpu.VMEM((SLOTS, rows, columns), jnp.bfloat16),
            pltpu.VMEM((SLOTS, rows, columns), jnp.bfloat16),
            pltpu.VMEM((2, 2, 4, 4, 4) + wpart.shape[1:], jnp.bfloat16),
            pltpu.VMEM((4, segs * rows, kv), jnp.bfloat16),
            pltpu.VMEM((4, segs * rows, kv), jnp.bfloat16),
            pltpu.VMEM((3, segs * rows, kv), jnp.bfloat16),
            pltpu.VMEM((3, segs * rows, kv), jnp.bfloat16),
            dma((SLOTS,)), dma((SLOTS,)),
            dma((CHUNKS, TZ)), dma((CHUNKS, TZ)), dma((CHUNKS, TZ)), dma((CHUNKS, TZ)),
            dma((SLOTS,)), dma((SLOTS,)),
            dma((TZ,)), dma((TZ,)),
            dma((2, 4)), dma((2, 4)), dma((2, 4)), dma((2, 4)), dma((2, 4)), dma((2, 4)),
            dma((4,)), dma((4,)), dma((3,)), dma((3,)),
        ],
        compiler_params=pltpu.CompilerParams(
            collective_id=0, has_side_effects=True, vmem_limit_bytes=48 * 2**20
        ),
        cost_estimate=pl.CostEstimate(flops=10**9, bytes_accessed=200 * 2**20, transcendentals=0),
        name="exchange",
    )(seg_of_group, group_of_seg, local_of_replica, x, down, upq, upkv, wpart)


def attend_kernel(live, q_ref, delta_ref, base_ref, cache_ref, bias_ref, out_ref):
    s = pl.program_id(0)
    heads = q_ref.shape[1] // HEAD_WIDTH
    wide = q_ref.shape[1]
    half = 8
    delta = delta_ref[0].astype(jnp.float32) * ADAPTER_SCALE
    q_all = (q_ref[...].astype(jnp.float32) + delta[:, :wide]).astype(jnp.bfloat16)
    fresh = (base_ref[...] + delta[:, wide:]).astype(jnp.bfloat16)
    rows = half * 2
    n = heads * rows
    row = lax.broadcasted_iota(jnp.int32, (n, half * CTX), 0)
    col = lax.broadcasted_iota(jnp.int32, (n, half * CTX), 1)
    same = (row % rows) // 2 == col // CTX
    row = lax.broadcasted_iota(jnp.int32, (n, rows), 0) % rows
    col = lax.broadcasted_iota(jnp.int32, (n, rows), 1)
    same_fresh = (row // 2 == col // 2) & (col <= row)
    scale = 1.0 / math.sqrt(HEAD_WIDTH)
    for h in range(2):
        at = slice(h * rows, (h + 1) * rows)
        q = jnp.concatenate(
            [q_all[at, g * HEAD_WIDTH : (g + 1) * HEAD_WIDTH] for g in range(heads)], axis=0
        )
        keys = cache_ref[h * half : (h + 1) * half, 0].reshape(half * CTX, HEAD_WIDTH)
        values = cache_ref[h * half : (h + 1) * half, 1].reshape(half * CTX, HEAD_WIDTH)
        new_keys = fresh[at, :HEAD_WIDTH]
        new_values = fresh[at, HEAD_WIDTH:]
        nt = (((1,), (1,)), ((), ()))
        old = lax.dot_general(q, keys, nt, preferred_element_type=jnp.float32) * scale
        new = lax.dot_general(q, new_keys, nt, preferred_element_type=jnp.float32) * scale
        old = jnp.where(same, old + bias_ref[0, h : h + 1], -jnp.inf)
        new = jnp.where(same_fresh, new, -jnp.inf)
        top = jnp.maximum(
            jnp.max(old, axis=1, keepdims=True), jnp.max(new, axis=1, keepdims=True)
        )
        old = jnp.exp(old - top)
        new = jnp.exp(new - top)
        total = jnp.sum(old, axis=1, keepdims=True) + jnp.sum(new, axis=1, keepdims=True)
        mixed = jnp.dot(old.astype(jnp.bfloat16), values, preferred_element_type=jnp.float32)
        mixed = mixed + jnp.dot(
            new.astype(jnp.bfloat16), new_values, preferred_element_type=jnp.float32
        )
        mixed = mixed / total
        out = jnp.concatenate([mixed[g * rows : (g + 1) * rows] for g in range(heads)], axis=1)
        place = h * half + lax.broadcasted_iota(jnp.int32, out.shape, 0) // 2
        out_ref[at, :] = jnp.where(place < live[s], out, 0.0).astype(jnp.bfloat16)


def attend(live, q, delta, base, cache, bias):
    segs = live.shape[0]
    rows, wide = q.shape
    per = rows // segs
    return pl.pallas_call(
        attend_kernel,
        grid_spec=pltpu.PrefetchScalarGridSpec(
            num_scalar_prefetch=1,
            grid=(segs,),
            in_specs=[
                pl.BlockSpec((per, wide), lambda s, _: (s, 0)),
                pl.BlockSpec((1,) + delta.shape[1:], lambda s, _: (s, 0, 0)),
                pl.BlockSpec((per, base.shape[1]), lambda s, _: (s, 0)),
                pl.BlockSpec((cache.shape[0] // segs,) + cache.shape[1:], lambda s, _: (s, 0, 0, 0)),
                pl.BlockSpec((1,) + bias.shape[1:], lambda s, _: (s, 0, 0)),
            ],
            out_specs=pl.BlockSpec((per, wide), lambda s, _: (s, 0)),
        ),
        out_shape=jax.ShapeDtypeStruct((rows, wide), jnp.bfloat16),
        compiler_params=pltpu.CompilerParams(vmem_limit_bytes=24 * 2**20),
        name="attend",
    )(live, q, delta, base, cache, bias)


def shards(
    normed_token_input,
    rotated_base_query,
    key_value_weight,
    key_value_cache,
    adapter_down_maps,
    query_up_maps,
    key_value_up_maps,
    adapter_storage_row,
    segment_adapter,
    segment_live_requests,
    cache_length,
):
    requests, tokens, features = normed_token_input.shape
    wide = rotated_base_query.shape[2]
    kv_wide = key_value_weight.shape[2]
    owned = adapter_down_maps.shape[0]
    replicas = lax.axis_size("replica")
    segs = segment_live_requests.shape[0]
    me = lax.axis_index("replica")

    adapter_ids = jnp.arange(adapter_storage_row.shape[0], dtype=jnp.int32)
    slot = jnp.sum(
        jnp.where(
            segment_adapter[:, None] == adapter_ids[None, :], adapter_storage_row[None, :], 0
        ),
        axis=1,
    ).reshape(replicas, segs)
    group, local = slot // owned, slot % owned
    group_of_seg = lax.dynamic_index_in_dim(group, me, 0, keepdims=False)
    group_ids = jnp.arange(replicas, dtype=jnp.int32)
    seg_ids = jnp.arange(segs, dtype=jnp.int32)
    seg_of_group = jnp.sum(
        jnp.where(group_of_seg[None, :] == group_ids[:, None], seg_ids[None, :], 0), axis=1
    )
    local_of_replica = jnp.sum(jnp.where(group == me, local, 0), axis=1)

    tensors = lax.axis_size("tensor")
    y, x, core = me // 8, (me // 2) % 4, me % 2
    place = core * 16 + jnp.where(lax.axis_index("tensor") < 4, y * 4 + x, x * 4 + y)
    by_place = key_value_weight.reshape(tensors, replicas, -1, 2, kv_wide)
    wpart = lax.dynamic_index_in_dim(by_place, place, 1, keepdims=False)
    wpart = wpart.reshape(tensors, wpart.shape[1], 2 * kv_wide)
    delta, base_kv = exchange(
        seg_of_group, group_of_seg, local_of_replica,
        normed_token_input.reshape(segs, requests * tokens // segs, features),
        adapter_down_maps, query_up_maps, key_value_up_maps, wpart,
    )
    spots = jnp.arange(CTX, dtype=jnp.int32)
    bias = jnp.where(spots[None, :] < cache_length[:, None], 0.0, -jnp.inf).astype(jnp.float32)
    out = attend(
        segment_live_requests, rotated_base_query.reshape(requests * tokens, wide), delta, base_kv,
        key_value_cache, bias.reshape(segs, 2, requests // segs // 2 * CTX),
    )
    return out.reshape(requests, tokens, wide)


def solution(mesh):
    return jax.shard_map(
        shards,
        mesh=mesh,
        in_specs=(
            P("replica", None, "tensor"),
            P("replica", None, "tensor"),
            P(None, None, "tensor"),
            P("replica", None, None, "tensor"),
            P("replica", None, "tensor"),
            P("replica", None, "tensor"),
            P("replica", None, None, "tensor"),
            P(),
            P(),
            P("replica"),
            P("replica"),
        ),
        out_specs=P("replica", None, "tensor"),
        check_vma=False,
    )
```

```python
import functools
import math

import jax
import jax.numpy as jnp
from jax import lax
from jax.experimental import pallas as pl
from jax.experimental.pallas import tpu as pltpu
from jax.sharding import PartitionSpec as P

HEAD_WIDTH = 128
CTX = 32
ADAPTER_SCALE = 0.5
MESH = pl.DeviceIdType.MESH

RINGS = (
    ((2, 2),),
    ((2, 1), (1, 2), (2, 3), (3, 2)),
    ((0, 2), (2, 0)),
    ((1, 1), (3, 3), (1, 3), (3, 1)),
    ((0, 1), (1, 0), (0, 3), (3, 0)),
)
OFFSETS = [(0, 0, 0)] + [(dy, dx, dc) for ring in RINGS for dc in (0, 1) for dy, dx in ring] + [(0, 0, 1)]
SLOTS = 32
CHUNKS = 4
PER = SLOTS // CHUNKS
TZ = 8


def packed(chunk, which, bits):
    total = 0
    for j in range(PER):
        total += OFFSETS[chunk * PER + j][which] << (bits * j)
    return total


PACK_Y = [packed(c, 0, 2) for c in range(CHUNKS)]
PACK_X = [packed(c, 1, 2) for c in range(CHUNKS)]
PACK_C = [packed(c, 2, 1) for c in range(CHUNKS)]


def offset(chunk, j):
    return (
        (PACK_Y[chunk] >> (2 * j)) & 3,
        (PACK_X[chunk] >> (2 * j)) & 3,
        (PACK_C[chunk] >> j) & 1,
    )


def moved(me, off, sign):
    y, x, c = me // 8, (me // 2) % 4, me % 2
    dy, dx, dc = off
    return ((y + 4 + sign * dy) % 4) * 8 + ((x + 4 + sign * dx) % 4) * 2 + (c + dc) % 2


def layer_kernel(
    seg_of_group, group_of_seg, local_of_replica, live, lengths,
    x_hbm, down_hbm, upq_hbm, upkv_hbm, q_hbm, cache_hbm, wpart_ref,
    out_ref,
    x_raw, down_ref, upq_ref, upkv_ref, q_raw, cache_ref, load_sem,
    x_ref, q_ref, base_ref, res, same,
    xs, xr, part, rs, ag, ds, dr, wall, right_out, right_in, left_out, left_in,
    x_send, x_recv, rs_send, rs_recv, ag_send, ag_recv, d_send, d_recv,
    wz_send, wz_recv, wp_send, wp_recv, ws_send, ws_recv, own_sem,
    right_send, right_recv, left_send, left_recv,
):
    me = lax.axis_index("replica")
    t = lax.axis_index("tensor")
    y, x, core = me // 8, (me // 2) % 4, me % 2

    barrier = pltpu.get_barrier_semaphore()

    def greet_plane(i, _):
        pl.semaphore_signal(barrier, inc=1, device_id=((me + i) % SLOTS, t), device_id_type=MESH)
        return 0

    def greet_z(i, _):
        pl.semaphore_signal(barrier, inc=1, device_id=(me, (t + i) % TZ), device_id_type=MESH)
        return 0

    lax.fori_loop(1, SLOTS, greet_plane, 0)
    lax.fori_loop(1, TZ, greet_z, 0)

    loads = [
        pltpu.make_async_copy(src, dst, load_sem.at[i])
        for i, (src, dst) in enumerate(
            [(x_hbm, x_raw), (down_hbm, down_ref), (upq_hbm, upq_ref), (upkv_hbm, upkv_ref),
             (cache_hbm, cache_ref), (q_hbm, q_raw)]
        )
    ]
    for load in loads:
        load.start()

    def x_copy(chunk, j):
        p = chunk * PER + j
        return pltpu.make_async_remote_copy(
            src_ref=xs.at[p], dst_ref=xr.at[p], send_sem=x_send.at[p], recv_sem=x_recv.at[p],
            device_id=(moved(me, offset(chunk, j), 1), t), device_id_type=MESH,
        )

    def d_copy(chunk, j):
        p = chunk * PER + j
        return pltpu.make_async_remote_copy(
            src_ref=ds.at[p], dst_ref=dr.at[p], send_sem=d_send.at[p], recv_sem=d_recv.at[p],
            device_id=(moved(me, offset(chunk, j), -1), t), device_id_type=MESH,
        )

    def rs_copy(chunk, u, sender):
        return pltpu.make_async_remote_copy(
            src_ref=part.at[chunk * PER + u], dst_ref=rs.at[chunk, sender],
            send_sem=rs_send.at[chunk, u], recv_sem=rs_recv.at[chunk, sender],
            device_id=(me, u), device_id_type=MESH,
        )

    def ag_copy(chunk, u, sender):
        return pltpu.make_async_remote_copy(
            src_ref=ag.at[chunk, sender], dst_ref=ag.at[chunk, sender],
            send_sem=ag_send.at[chunk, u], recv_sem=ag_recv.at[chunk, sender],
            device_id=(me, u), device_id_type=MESH,
        )

    def pair_of(share):
        quarter = share // 2
        on_y = quarter // 2
        b = (jnp.where(on_y == 1, y, x) + quarter % 2) % 2
        step = 1 + 2 * b
        partner = jnp.where(
            on_y == 1, ((y + step) % 4) * 8 + x * 2 + core, y * 8 + ((x + step) % 4) * 2 + core
        )
        return b, partner

    def wz_copy(u, sender):
        return pltpu.make_async_remote_copy(
            src_ref=wpart_ref.at[u], dst_ref=wall.at[sender, core, pair_of(sender)[0]],
            send_sem=wz_send.at[u], recv_sem=wz_recv.at[sender],
            device_id=(me, u), device_id_type=MESH,
        )

    def wp_copy(u):
        b, partner = pair_of(u)
        piece = wall.at[u, core, b]
        return pltpu.make_async_remote_copy(
            src_ref=piece, dst_ref=piece, send_sem=wp_send.at[u], recv_sem=wp_recv.at[u],
            device_id=(partner, t), device_id_type=MESH,
        )

    def ws_copy(u, k):
        b = pair_of(u)[0]
        piece = wall.at[u, core, (b + k) % 2]
        return pltpu.make_async_remote_copy(
            src_ref=piece, dst_ref=piece, send_sem=ws_send.at[u, k], recv_sem=ws_recv.at[u, k],
            device_id=(y * 8 + x * 2 + 1 - core, t), device_id_type=MESH,
        )

    own_weight = pltpu.make_async_copy(
        wpart_ref.at[t], wall.at[t, core, pair_of(t)[0]], own_sem.at[0]
    )

    def weight_z():
        for d in (4, 3, 5, 2, 6, 1, 7):
            wz_copy((t + d) % TZ, t).start()
        own_weight.start()

    steps = ((4, 5), (3, 6), (2, 7), (1,), (0,))

    def weight_first(s):
        for d in steps[s]:
            u = (t + d) % TZ
            if d:
                wz_copy(t, u).wait_recv()
            else:
                own_weight.wait()
            wp_copy(u).start()
            ws_copy(u, 0).start()

    def weight_second(s):
        for d in steps[s]:
            u = (t + d) % TZ
            wp_copy(u).wait_recv()
            ws_copy(u, 1).start()

    def weight_third(s):
        for d in steps[s]:
            u = (t + d) % TZ
            ws_copy(u, 0).wait_recv()
            ws_copy(u, 1).wait_recv()

    tall = 256
    segs_of_tile = tall // x_ref.shape[1]
    tiles = x_ref.shape[0] // segs_of_tile

    def right_copy(s, i):
        at = pl.ds(i * tall, tall)
        return pltpu.make_async_remote_copy(
            src_ref=right_out.at[s, at], dst_ref=right_in.at[s, at],
            send_sem=right_send.at[s, i], recv_sem=right_recv.at[s, i],
            device_id=(me, (t + 1) % TZ), device_id_type=MESH,
        )

    def left_copy(s, i):
        at = pl.ds(i * tall, tall)
        return pltpu.make_async_remote_copy(
            src_ref=left_out.at[s, at], dst_ref=left_in.at[s, at],
            send_sem=left_send.at[s, i], recv_sem=left_recv.at[s, i],
            device_id=(me, (t + TZ - 1) % TZ), device_id_type=MESH,
        )

    def base_part(share, i):
        w = wall[share].reshape(x_ref.shape[2], base_ref.shape[2])
        rows = x_ref[pl.ds(i * segs_of_tile, segs_of_tile)].reshape(tall, x_ref.shape[2])
        return jnp.dot(rows, w, preferred_element_type=jnp.float32)

    def ring(s):
        def tile(i, _):
            at = pl.ds(i * tall, tall)
            if s < 4:
                value = base_part((t + 4 - s) % TZ, i)
                if s > 0:
                    right_copy(s - 1, i).wait_recv()
                    value = value + right_in[s - 1, at].astype(jnp.float32)
                right_out[s, at] = value.astype(jnp.bfloat16)
                right_copy(s, i).start()
            if s < 3:
                value = base_part((t + TZ - 3 + s) % TZ, i)
                if s > 0:
                    left_copy(s - 1, i).wait_recv()
                    value = value + left_in[s - 1, at].astype(jnp.float32)
                left_out[s, at] = value.astype(jnp.bfloat16)
                left_copy(s, i).start()
            return 0

        lax.fori_loop(0, tiles, tile, 0)

    def ring_end():
        def tile(i, _):
            at = pl.ds(i * tall, tall)
            value = base_part(t, i)
            left_copy(2, i).wait_recv()
            right_copy(3, i).wait_recv()
            value = value + right_in[3, at].astype(jnp.float32) + left_in[2, at].astype(jnp.float32)
            base_ref[pl.ds(i * segs_of_tile, segs_of_tile)] = value.reshape(
                segs_of_tile, base_ref.shape[1], base_ref.shape[2]
            )
            return 0

        lax.fori_loop(0, tiles, tile, 0)

    per_seg = x_raw.shape[0] // x_ref.shape[0]

    def by_rows(raw, ref):
        def one(s, _):
            ref[s] = raw[pl.ds(s * per_seg, per_seg)].reshape(ref.shape[1:])
            return 0

        lax.fori_loop(0, ref.shape[0], one, 0)

    loads[0].wait()
    by_rows(x_raw, x_ref)
    for chunk in range(CHUNKS):
        def fill(j, _, chunk=chunk):
            group = moved(me, offset(chunk, j), 1)
            xs[chunk * PER + j] = x_ref[seg_of_group[group]]
            return 0

        lax.fori_loop(0, PER, fill, 0)
    pl.semaphore_wait(barrier, SLOTS - 1 + TZ - 1)
    weight_z()

    def send_inputs(chunk):
        def send(j, _):
            x_copy(chunk, j).start()
            return 0

        lax.fori_loop(1 if chunk == 0 else 0, PER, send, 0)

    def shrink_parts(chunk):
        def one(j, _):
            p = chunk * PER + j
            rows = xs[0] if chunk == 0 and isinstance(j, int) else xr[p]
            w = down_ref[local_of_replica[moved(me, offset(chunk, j), -1)]]
            part[p] = lax.dot_general(
                rows, w, (((1,), (1,)), ((), ())), preferred_element_type=jnp.float32
            ).astype(jnp.bfloat16)
            return 0

        def arrived(j, _):
            x_copy(chunk, j).wait_recv()
            return one(j, 0)

        if chunk == 0:
            one(0, 0)
        lax.fori_loop(1 if chunk == 0 else 0, PER, arrived, 0)

        def send(i, _):
            rs_copy(chunk, (t + i) % TZ, t).start()
            return 0

        lax.fori_loop(1, TZ, send, 0)

    def add_up(chunk):
        def wait(i, _):
            rs_copy(chunk, t, (t + TZ - i) % TZ).wait_recv()
            return 0

        lax.fori_loop(1, TZ, wait, 0)
        rs[chunk, t] = part[chunk * PER + t]
        total = rs[chunk, 0].astype(jnp.float32)
        for u in range(1, TZ):
            total = total + rs[chunk, u].astype(jnp.float32)
        ag[chunk, t] = total.astype(jnp.bfloat16)

        def send(i, _):
            ag_copy(chunk, (t + i) % TZ, t).start()
            return 0

        lax.fori_loop(1, TZ, send, 0)

    def give_back(chunk):
        def wait(i, _):
            ag_copy(chunk, t, (t + TZ - i) % TZ).wait_recv()
            return 0

        lax.fori_loop(1, TZ, wait, 0)

        def deltas(j):
            a = local_of_replica[moved(me, offset(chunk, j), -1)]
            shrink = ag[chunk, j]
            q = jnp.dot(shrink[:, 0:64], upq_ref[a], preferred_element_type=jnp.float32)
            k = jnp.dot(shrink[:, 64:128], upkv_ref[a, 0], preferred_element_type=jnp.float32)
            v = jnp.dot(shrink[:, 128:192], upkv_ref[a, 1], preferred_element_type=jnp.float32)
            return jnp.concatenate([q, k, v], axis=1).astype(jnp.bfloat16)

        def one(j, _):
            ds[chunk * PER + j] = deltas(j)
            d_copy(chunk, j).start()
            return 0

        if chunk == 0:
            dr[0] = deltas(0)
        lax.fori_loop(1 if chunk == 0 else 0, PER, one, 0)

    half = 8
    heads = q_ref.shape[2] // HEAD_WIDTH
    wide = q_ref.shape[2]
    rows = half * 2
    n = heads * rows
    unit = math.log2(math.e) / math.sqrt(HEAD_WIDTH)

    old_keys = half * CTX
    all_keys = same.shape[1]

    def prepare():
        row = lax.broadcasted_iota(jnp.int32, same.shape, 0) % rows
        col = lax.broadcasted_iota(jnp.int32, same.shape, 1)
        new = col - old_keys
        old_fits = jnp.where(row // 2 == col // CTX, 0.0, -jnp.inf)
        new_fits = jnp.where((row // 2 == new // 2) & (new <= row), 0.0, -jnp.inf)
        same[...] = jnp.where(new < 0, old_fits, new_fits)
        loads[5].wait()
        by_rows(q_raw, q_ref)

    def attend(chunk):
        spot = lax.broadcasted_iota(jnp.int32, (1, old_keys), 1)
        owner, nth = spot // CTX, spot % CTX
        pad = jnp.zeros((all_keys - old_keys - rows, HEAD_WIDTH), jnp.bfloat16)
        ones = jnp.ones((all_keys, HEAD_WIDTH), jnp.bfloat16)
        no_bias = jnp.zeros((1, all_keys - old_keys), jnp.float32)

        def slot(j):
            group = moved(me, offset(chunk, j), 1)
            seg = seg_of_group[group]
            delta = dr[chunk * PER + j].astype(jnp.float32) * ADAPTER_SCALE
            q_all = (q_ref[seg].astype(jnp.float32) + delta[:, :wide]).astype(jnp.bfloat16)
            fresh = (base_ref[seg] + delta[:, wide:]).astype(jnp.bfloat16)
            outs = []
            for h in range(2):
                at = slice(h * rows, (h + 1) * rows)
                q = jnp.concatenate(
                    [q_all[at, g * HEAD_WIDTH : (g + 1) * HEAD_WIDTH] for g in range(heads)], axis=0
                )
                keys = cache_ref[seg, h * half : (h + 1) * half, 0].reshape(old_keys, HEAD_WIDTH)
                values = cache_ref[seg, h * half : (h + 1) * half, 1].reshape(old_keys, HEAD_WIDTH)
                keys = jnp.concatenate([keys, fresh[at, :HEAD_WIDTH], pad], axis=0)
                values = jnp.concatenate([values, fresh[at, HEAD_WIDTH:], pad], axis=0)
                values = jnp.concatenate([values, ones], axis=1)
                ends = jnp.zeros(spot.shape, jnp.int32)
                for i in range(half):
                    ends = jnp.where(owner == i, lengths[seg * 2 * half + h * half + i], ends)
                bias = jnp.concatenate([jnp.where(nth < ends, 0.0, -jnp.inf), no_bias], axis=1)
                scores = lax.dot_general(
                    q, keys, (((1,), (1,)), ((), ())), preferred_element_type=jnp.float32
                )
                scores = scores + (same[...] + bias)
                lifted = jnp.exp2((scores - jnp.max(scores, axis=1, keepdims=True)) * unit)
                mixed = jnp.dot(lifted.astype(jnp.bfloat16), values, preferred_element_type=jnp.float32)
                mixed = mixed[:, :HEAD_WIDTH] / mixed[:, HEAD_WIDTH:]
                out = jnp.concatenate(
                    [mixed[g * rows : (g + 1) * rows] for g in range(heads)], axis=1
                )
                place = h * half + lax.broadcasted_iota(jnp.int32, out.shape, 0) // 2
                outs.append(jnp.where(place < live[seg], out, 0.0).astype(jnp.bfloat16))
            return group, jnp.concatenate(outs, axis=0)

        def pair(i, _):
            for b in range(2):
                if chunk == 0 and b == 0:
                    @pl.when(i > 0)
                    def _():
                        d_copy(chunk, 2 * i).wait_recv()
                else:
                    d_copy(chunk, 2 * i + b).wait_recv()
            done = [slot(2 * i + b) for b in range(2)]
            for group, out in done:
                res[group] = out.reshape(res.shape[1:])
            return 0

        lax.fori_loop(0, PER // 2, pair, 0)

    send_inputs(0)
    send_inputs(1)
    prepare()
    loads[1].wait()
    shrink_parts(0)
    weight_first(0)
    send_inputs(2)
    send_inputs(3)
    loads[2].wait()
    loads[3].wait()
    weight_second(0)
    weight_first(1)
    add_up(0)
    weight_third(0)
    ring(0)
    shrink_parts(1)
    weight_second(1)
    weight_first(2)
    give_back(0)
    weight_third(1)
    ring(1)
    add_up(1)
    shrink_parts(2)
    weight_second(2)
    weight_first(3)
    weight_first(4)
    shrink_parts(3)
    add_up(2)
    give_back(1)
    weight_third(2)
    ring(2)
    weight_second(3)
    weight_second(4)
    add_up(3)
    give_back(2)
    weight_third(3)
    ring(3)
    give_back(3)
    weight_third(4)
    ring_end()
    loads[4].wait()
    for chunk in range(CHUNKS):
        attend(chunk)

    def gather(s, _):
        out_ref[pl.ds(s * per_seg, per_seg)] = res[group_of_seg[s]]
        return 0

    lax.fori_loop(0, x_ref.shape[0], gather, 0)

    for chunk in range(CHUNKS):
        def settle(j, _, chunk=chunk):
            x_copy(chunk, j).wait_send()
            d_copy(chunk, j).wait_send()
            return 0

        lax.fori_loop(1 if chunk == 0 else 0, PER, settle, 0)

        def settle_z(i, _, chunk=chunk):
            rs_copy(chunk, (t + i) % TZ, t).wait_send()
            ag_copy(chunk, (t + i) % TZ, t).wait_send()
            return 0

        lax.fori_loop(1, TZ, settle_z, 0)

    def settle_w(i, _):
        wz_copy((t + i) % TZ, t).wait_send()
        return 0

    lax.fori_loop(1, TZ, settle_w, 0)
    def settle_shares(u, _):
        wp_copy(u).wait_send()
        ws_copy(u, 0).wait_send()
        ws_copy(u, 1).wait_send()
        return 0

    lax.fori_loop(0, TZ, settle_shares, 0)

    def settle_ring(i, _):
        for s in range(4):
            right_copy(s, i).wait_send()
        for s in range(3):
            left_copy(s, i).wait_send()
        return 0

    lax.fori_loop(0, tiles, settle_ring, 0)


def layer(tables, x, down, upq, upkv, q, cache, wpart):
    segs = tables[1].shape[0]
    tokens, features = x.shape[1:]
    per_seg = x.shape[0] // segs
    rows = per_seg * tokens
    ranks = down.shape[1]
    kv = wpart.shape[2]
    wide = q.shape[2]
    columns = wide + kv
    smem = pl.BlockSpec(memory_space=pltpu.SMEM)
    vmem = pl.BlockSpec(memory_space=pltpu.VMEM)
    hbm = pl.BlockSpec(memory_space=pltpu.HBM)
    dma = pltpu.SemaphoreType.DMA
    tiles = segs * rows // 256
    half_rows = rows // 2 * (wide // HEAD_WIDTH)
    loaded = [x, down, upq, upkv, q, cache]

    def room(*shape, dtype=jnp.bfloat16):
        return pltpu.VMEM(shape, dtype)

    return pl.pallas_call(
        layer_kernel,
        out_shape=jax.ShapeDtypeStruct(q.shape, jnp.bfloat16),
        in_specs=[smem] * len(tables) + [hbm] * (len(loaded) + 1),
        out_specs=vmem,
        scratch_shapes=[room(*a.shape) for a in loaded]
        + [
            dma((len(loaded),)),
            room(segs, rows, features),
            room(segs, rows, wide),
            room(segs, rows, kv, dtype=jnp.float32),
            room(SLOTS, per_seg, tokens, wide),
            room(half_rows, rows // 4 * CTX + 128, dtype=jnp.float32),
            room(SLOTS, rows, features),
            room(SLOTS, rows, features),
            room(SLOTS, rows, ranks),
            room(CHUNKS, TZ, rows, ranks),
            room(CHUNKS, TZ, rows, ranks),
            room(SLOTS, rows, columns),
            room(SLOTS, rows, columns),
            room(TZ, 2, 2, *wpart.shape[1:]),
            room(4, segs * rows, kv),
            room(4, segs * rows, kv),
            room(3, segs * rows, kv),
            room(3, segs * rows, kv),
            dma((SLOTS,)), dma((SLOTS,)),
            dma((CHUNKS, TZ)), dma((CHUNKS, TZ)), dma((CHUNKS, TZ)), dma((CHUNKS, TZ)),
            dma((SLOTS,)), dma((SLOTS,)),
            dma((TZ,)), dma((TZ,)),
            dma((TZ,)), dma((TZ,)), dma((TZ, 2)), dma((TZ, 2)), dma((1,)),
            dma((4, tiles)), dma((4, tiles)), dma((3, tiles)), dma((3, tiles)),
        ],
        compiler_params=pltpu.CompilerParams(
            collective_id=0, has_side_effects=True, vmem_limit_bytes=52 * 2**20
        ),
        name="layer",
    )(*tables, *loaded, wpart)


def shards(
    normed_token_input,
    rotated_base_query,
    key_value_weight,
    key_value_cache,
    adapter_down_maps,
    query_up_maps,
    key_value_up_maps,
    adapter_storage_row,
    segment_adapter,
    segment_live_requests,
    cache_length,
):
    requests, tokens, features = normed_token_input.shape
    wide = rotated_base_query.shape[2]
    kv_wide = key_value_weight.shape[2]
    owned = adapter_down_maps.shape[0]
    replicas = lax.axis_size("replica")
    segs = segment_live_requests.shape[0]
    me = lax.axis_index("replica")

    adapter_ids = jnp.arange(adapter_storage_row.shape[0], dtype=jnp.int32)
    slot = jnp.sum(
        jnp.where(
            segment_adapter[:, None] == adapter_ids[None, :], adapter_storage_row[None, :], 0
        ),
        axis=1,
    ).reshape(replicas, segs)
    group, local = lax.div(slot, owned), lax.rem(slot, owned)
    group_of_seg = lax.dynamic_index_in_dim(group, me, 0, keepdims=False)
    group_ids = jnp.arange(replicas, dtype=jnp.int32)
    seg_ids = jnp.arange(segs, dtype=jnp.int32)
    seg_of_group = jnp.sum(
        jnp.where(group_of_seg[None, :] == group_ids[:, None], seg_ids[None, :], 0), axis=1
    )
    local_of_replica = jnp.sum(jnp.where(group == me, local, 0), axis=1)

    tensors = lax.axis_size("tensor")
    y, x, core = me // 8, (me // 2) % 4, me % 2
    quarter = lax.axis_index("tensor") // 2
    b = (jnp.where(quarter // 2 == 1, y, x) + quarter % 2) % 2
    by_place = key_value_weight.reshape(tensors, 4, -1, 2, kv_wide)
    wpart = lax.dynamic_index_in_dim(by_place, core * 2 + b, 1, keepdims=False)
    wpart = wpart.reshape(tensors, wpart.shape[1], 2 * kv_wide)
    return layer(
        (seg_of_group, group_of_seg, local_of_replica, segment_live_requests, cache_length),
        normed_token_input, adapter_down_maps, query_up_maps, key_value_up_maps,
        rotated_base_query,
        key_value_cache.reshape((segs, requests // segs) + key_value_cache.shape[1:]),
        wpart,
    )


def solution(mesh):
    return jax.shard_map(
        shards,
        mesh=mesh,
        in_specs=(
            P("replica", None, "tensor"),
            P("replica", None, "tensor"),
            P(None, None, "tensor"),
            P("replica", None, None, "tensor"),
            P("replica", None, "tensor"),
            P("replica", None, "tensor"),
            P("replica", None, None, "tensor"),
            P(),
            P(),
            P("replica"),
            P("replica"),
        ),
        out_specs=P("replica", None, "tensor"),
        check_vma=False,
    )
```

```python
import functools
import math

import jax
import jax.numpy as jnp
from jax import lax
from jax.experimental import pallas as pl
from jax.experimental.pallas import tpu as pltpu
from jax.sharding import PartitionSpec as P

HEAD_WIDTH = 128
CTX = 32
ADAPTER_SCALE = 0.5
MESH = pl.DeviceIdType.MESH

RINGS = (
    ((2, 2),),
    ((2, 1), (1, 2), (2, 3), (3, 2)),
    ((0, 2), (2, 0)),
    ((1, 1), (3, 3), (1, 3), (3, 1)),
    ((0, 1), (1, 0), (0, 3), (3, 0)),
)
OFFSETS = [(0, 0, 0)] + [(dy, dx, dc) for ring in RINGS for dc in (0, 1) for dy, dx in ring] + [(0, 0, 1)]
SLOTS = 32
CHUNKS = 4
PER = SLOTS // CHUNKS
TZ = 8


def packed(chunk, which, bits):
    total = 0
    for j in range(PER):
        total += OFFSETS[chunk * PER + j][which] << (bits * j)
    return total


PACK_Y = [packed(c, 0, 2) for c in range(CHUNKS)]
PACK_X = [packed(c, 1, 2) for c in range(CHUNKS)]
PACK_C = [packed(c, 2, 1) for c in range(CHUNKS)]


def offset(chunk, j):
    return (
        (PACK_Y[chunk] >> (2 * j)) & 3,
        (PACK_X[chunk] >> (2 * j)) & 3,
        (PACK_C[chunk] >> j) & 1,
    )


def moved(me, off, sign):
    y, x, c = me // 8, (me // 2) % 4, me % 2
    dy, dx, dc = off
    return ((y + 4 + sign * dy) % 4) * 8 + ((x + 4 + sign * dx) % 4) * 2 + (c + dc) % 2


def layer_kernel(
    seg_of_group, group_of_seg, local_of_replica, live, lengths,
    x_hbm, down_hbm, upq_hbm, upkv_hbm, q_hbm, cache_hbm, w_hbm,
    out_ref,
    x_raw, down_ref, upq_ref, upkv_ref, q_raw, cache_ref, load_sem,
    x_ref, q_ref, base_ref, same,
    xs, xr, part, rs, ag, ds, dr, wall, right_out, right_in, left_out, left_in, wnow,
    x_send, x_recv, rs_send, rs_recv, ag_send, ag_recv, d_send, d_recv,
    wz_send, wz_recv, wp_send, wp_recv, ws_send, ws_recv, own_sem,
    right_send, right_recv, left_send, left_recv,
):
    me = lax.axis_index("replica")
    t = lax.axis_index("tensor")
    y, x, core = me // 8, (me // 2) % 4, me % 2

    barrier = pltpu.get_barrier_semaphore()

    def greet_plane(i, _):
        pl.semaphore_signal(barrier, inc=1, device_id=((me + i) % SLOTS, t), device_id_type=MESH)
        return 0

    def greet_z(i, _):
        pl.semaphore_signal(barrier, inc=1, device_id=(me, (t + i) % TZ), device_id_type=MESH)
        return 0

    lax.fori_loop(1, SLOTS, greet_plane, 0)
    lax.fori_loop(1, TZ, greet_z, 0)

    loads = [
        pltpu.make_async_copy(src, dst, load_sem.at[i])
        for i, (src, dst) in enumerate(
            [(x_hbm, x_raw), (down_hbm, down_ref), (upq_hbm, upq_ref), (upkv_hbm, upkv_ref),
             (cache_hbm, cache_ref), (q_hbm, q_raw)]
        )
    ]
    for load in loads:
        load.start()

    def x_copy(chunk, j):
        p = chunk * PER + j
        return pltpu.make_async_remote_copy(
            src_ref=xs.at[p], dst_ref=xr.at[p], send_sem=x_send.at[p], recv_sem=x_recv.at[p],
            device_id=(moved(me, offset(chunk, j), 1), t), device_id_type=MESH,
        )

    def d_copy(chunk, j):
        p = chunk * PER + j
        return pltpu.make_async_remote_copy(
            src_ref=ds.at[p], dst_ref=dr.at[me], send_sem=d_send.at[p], recv_sem=d_recv.at[p],
            device_id=(moved(me, offset(chunk, j), -1), t), device_id_type=MESH,
        )

    def rs_copy(chunk, u, sender):
        return pltpu.make_async_remote_copy(
            src_ref=part.at[chunk * PER + u], dst_ref=rs.at[chunk, sender],
            send_sem=rs_send.at[chunk, u], recv_sem=rs_recv.at[chunk, sender],
            device_id=(me, u), device_id_type=MESH,
        )

    def ag_copy(chunk, u, sender):
        return pltpu.make_async_remote_copy(
            src_ref=ag.at[chunk, sender], dst_ref=ag.at[chunk, sender],
            send_sem=ag_send.at[chunk, u], recv_sem=ag_recv.at[chunk, sender],
            device_id=(me, u), device_id_type=MESH,
        )

    def pair_of(share):
        quarter = share // 2
        on_y = quarter // 2
        b = (jnp.where(on_y == 1, y, x) + quarter % 2) % 2
        step = 1 + 2 * b
        partner = jnp.where(
            on_y == 1, ((y + step) % 4) * 8 + x * 2 + core, y * 8 + ((x + step) % 4) * 2 + core
        )
        return b, partner

    def own_rows(u):
        place = core * 2 + pair_of(t)[0]
        return w_hbm.at[pl.ds((u * 4 + place) * wall.shape[3], wall.shape[3])]

    def wz_copy(u, sender):
        return pltpu.make_async_remote_copy(
            src_ref=own_rows(u), dst_ref=wall.at[sender, core, pair_of(sender)[0]],
            send_sem=wz_send.at[u], recv_sem=wz_recv.at[sender],
            device_id=(me, u), device_id_type=MESH,
        )

    def wp_copy(u):
        b, partner = pair_of(u)
        piece = wall.at[u, core, b]
        return pltpu.make_async_remote_copy(
            src_ref=piece, dst_ref=piece, send_sem=wp_send.at[u], recv_sem=wp_recv.at[u],
            device_id=(partner, t), device_id_type=MESH,
        )

    def ws_copy(u, k):
        b = pair_of(u)[0]
        piece = wall.at[u, core, (b + k) % 2]
        return pltpu.make_async_remote_copy(
            src_ref=piece, dst_ref=piece, send_sem=ws_send.at[u, k], recv_sem=ws_recv.at[u, k],
            device_id=(y * 8 + x * 2 + 1 - core, t), device_id_type=MESH,
        )

    own_weight = pltpu.make_async_copy(
        own_rows(t), wall.at[t, core, pair_of(t)[0]], own_sem.at[0]
    )

    def weight_z(*hops):
        for d in hops:
            wz_copy((t + d) % TZ, t).start()

    steps = ((4,), (3, 5), (2, 6), (1, 7), (0,))

    def weight_first(s):
        for d in steps[s]:
            u = (t + d) % TZ
            if d:
                wz_copy(t, u).wait_recv()
            else:
                own_weight.wait()
            wp_copy(u).start()
            ws_copy(u, 0).start()

    def weight_second(s):
        for d in steps[s]:
            u = (t + d) % TZ
            wp_copy(u).wait_recv()
            ws_copy(u, 1).start()

    def weight_third(s):
        for d in steps[s]:
            u = (t + d) % TZ
            ws_copy(u, 0).wait_recv()
            ws_copy(u, 1).wait_recv()

    tall = 256
    segs_of_tile = tall // x_ref.shape[1]
    tiles = x_ref.shape[0] // segs_of_tile

    def right_copy(s, i):
        at = pl.ds(i * tall, tall)
        return pltpu.make_async_remote_copy(
            src_ref=right_out.at[s, at], dst_ref=right_in.at[s, at],
            send_sem=right_send.at[s, i], recv_sem=right_recv.at[s, i],
            device_id=(me, (t + 1) % TZ), device_id_type=MESH,
        )

    def left_copy(s, i):
        at = pl.ds(i * tall, tall)
        return pltpu.make_async_remote_copy(
            src_ref=left_out.at[s, at], dst_ref=left_in.at[s, at],
            send_sem=left_send.at[s, i], recv_sem=left_recv.at[s, i],
            device_id=(me, (t + TZ - 1) % TZ), device_id_type=MESH,
        )

    def weight_of(share, k):
        wide_rows = wall[share].reshape((x_ref.shape[2],) + wall.shape[4:])
        wnow[k] = wide_rows.reshape(wnow.shape[1:])

    def base_part(k, i):
        rows = x_ref[pl.ds(i * segs_of_tile, segs_of_tile)].reshape(tall, x_ref.shape[2])
        return jnp.dot(rows, wnow[k], preferred_element_type=jnp.float32)

    def pass_right(s, i, value):
        at = pl.ds(i * tall, tall)
        if s > i:
            right_copy(s - 1, i).wait_recv()
            value = value + right_in[s - 1, at].astype(jnp.float32)
        right_out[s, at] = value.astype(jnp.bfloat16)
        right_copy(s, i).start()

    def pass_left(s, i, value):
        at = pl.ds(i * tall, tall)
        if s > 1 - i:
            left_copy(s - 1, i).wait_recv()
            value = value + left_in[s - 1, at].astype(jnp.float32)
        left_out[s, at] = value.astype(jnp.bfloat16)
        left_copy(s, i).start()

    def ring(s):
        for k, d in enumerate(steps[s]):
            weight_of((t + d) % TZ, k)
        if s == 0:
            pass_right(0, 0, base_part(0, 0))
            pass_left(0, 1, base_part(0, 1))
        else:
            for i in range(tiles):
                pass_right(s, i, base_part(0, i))
                pass_left(s, i, base_part(1, i))

    def ring_end():
        weight_of(t, 0)
        for i in range(tiles):
            at = pl.ds(i * tall, tall)
            value = base_part(0, i)
            left_copy(3, i).wait_recv()
            right_copy(3, i).wait_recv()
            value = value + right_in[3, at].astype(jnp.float32) + left_in[3, at].astype(jnp.float32)
            base_ref[pl.ds(i * segs_of_tile, segs_of_tile)] = value.reshape(
                segs_of_tile, base_ref.shape[1], base_ref.shape[2]
            )

    per_seg = x_raw.shape[0] // x_ref.shape[0]

    def by_rows(raw, ref):
        def one(s, _):
            ref[s] = raw[pl.ds(s * per_seg, per_seg)].reshape(ref.shape[1:])
            return 0

        lax.fori_loop(0, ref.shape[0], one, 0)

    loads[0].wait()
    by_rows(x_raw, x_ref)
    for chunk in range(CHUNKS):
        def fill(j, _, chunk=chunk):
            group = moved(me, offset(chunk, j), 1)
            xs[chunk * PER + j] = x_ref[seg_of_group[group]]
            return 0

        lax.fori_loop(0, PER, fill, 0)
    pl.semaphore_wait(barrier, SLOTS - 1 + TZ - 1)
    own_weight.start()

    def send_inputs(chunk):
        def send(j, _):
            x_copy(chunk, j).start()
            return 0

        lax.fori_loop(1 if chunk == 0 else 0, PER, send, 0)

    def packed_shrink(shrink):
        mid = shrink.shape[0] // 2
        value = jnp.concatenate([shrink[:mid, 128:], shrink[mid:, 128:]], axis=1)
        return jnp.concatenate([shrink[:, :128], value], axis=0)

    def shrink_parts(chunk):
        def one(j, _):
            p = chunk * PER + j
            rows = xs[0] if chunk == 0 and isinstance(j, int) else xr[p]
            w = down_ref[local_of_replica[moved(me, offset(chunk, j), -1)]]
            shrink = lax.dot_general(
                rows, w, (((1,), (1,)), ((), ())), preferred_element_type=jnp.float32
            )
            part[p] = packed_shrink(shrink).astype(jnp.bfloat16)
            return 0

        def arrived(j, _):
            x_copy(chunk, j).wait_recv()
            return one(j, 0)

        if chunk == 0:
            one(0, 0)
        lax.fori_loop(1 if chunk == 0 else 0, PER, arrived, 0)

        def send(i, _):
            rs_copy(chunk, (t + i) % TZ, t).start()
            return 0

        lax.fori_loop(1, TZ, send, 0)

    def add_up(chunk):
        def wait(i, _):
            rs_copy(chunk, t, (t + TZ - i) % TZ).wait_recv()
            return 0

        lax.fori_loop(1, TZ, wait, 0)
        rs[chunk, t] = part[chunk * PER + t]
        total = rs[chunk, 0].astype(jnp.float32)
        for u in range(1, TZ):
            total = total + rs[chunk, u].astype(jnp.float32)
        ag[chunk, t] = total.astype(jnp.bfloat16)

        def send(i, _):
            ag_copy(chunk, (t + i) % TZ, t).start()
            return 0

        lax.fori_loop(1, TZ, send, 0)

    def give_back(chunk):
        def wait(i, _):
            ag_copy(chunk, t, (t + TZ - i) % TZ).wait_recv()
            return 0

        lax.fori_loop(1, TZ, wait, 0)

        def deltas(j):
            a = local_of_replica[moved(me, offset(chunk, j), -1)]
            both = ag[chunk, j]
            mid = both.shape[0] // 3
            shrink, value = both[: 2 * mid], both[2 * mid :]
            value = jnp.concatenate([value[:, :64], value[:, 64:]], axis=0)
            q = jnp.dot(shrink[:, 0:64], upq_ref[a], preferred_element_type=jnp.float32)
            k = jnp.dot(shrink[:, 64:128], upkv_ref[a, 0], preferred_element_type=jnp.float32)
            v = jnp.dot(value, upkv_ref[a, 1], preferred_element_type=jnp.float32)
            return jnp.concatenate([q, k, v], axis=1).astype(jnp.bfloat16)

        def one(j, _):
            ds[chunk * PER + j] = deltas(j)
            d_copy(chunk, j).start()
            return 0

        if chunk == 0:
            dr[me] = deltas(0)
        lax.fori_loop(1 if chunk == 0 else 0, PER, one, 0)

    half = 8
    heads = q_ref.shape[2] // HEAD_WIDTH
    wide = q_ref.shape[2]
    rows = half * 2
    n = heads * rows
    unit = math.log2(math.e) / math.sqrt(HEAD_WIDTH)

    old_keys = half * CTX
    all_keys = same.shape[1]

    def prepare():
        row = lax.broadcasted_iota(jnp.int32, same.shape, 0) % rows
        col = lax.broadcasted_iota(jnp.int32, same.shape, 1)
        new = col - old_keys
        old_fits = jnp.where(row // 2 == col // CTX, 0.0, -jnp.inf)
        new_fits = jnp.where((row // 2 == new // 2) & (new <= row), 0.0, -jnp.inf)
        same[...] = jnp.where(new < 0, old_fits, new_fits)
        loads[5].wait()
        by_rows(q_raw, q_ref)

    def attend():
        spot = lax.broadcasted_iota(jnp.int32, (1, old_keys), 1)
        owner, nth = spot // CTX, spot % CTX
        pad = jnp.zeros((all_keys - old_keys - rows, HEAD_WIDTH), jnp.bfloat16)
        ones = jnp.ones((all_keys, HEAD_WIDTH), jnp.bfloat16)
        no_bias = jnp.zeros((1, all_keys - old_keys), jnp.float32)

        def segment(seg):
            delta = dr[group_of_seg[seg]].astype(jnp.float32) * ADAPTER_SCALE
            q_all = (q_ref[seg].astype(jnp.float32) + delta[:, :wide]).astype(jnp.bfloat16)
            fresh = (base_ref[seg] + delta[:, wide:]).astype(jnp.bfloat16)
            outs = []
            for h in range(2):
                at = slice(h * rows, (h + 1) * rows)
                q = jnp.concatenate(
                    [q_all[at, g * HEAD_WIDTH : (g + 1) * HEAD_WIDTH] for g in range(heads)], axis=0
                )
                keys = cache_ref[seg, h * half : (h + 1) * half, 0].reshape(old_keys, HEAD_WIDTH)
                values = cache_ref[seg, h * half : (h + 1) * half, 1].reshape(old_keys, HEAD_WIDTH)
                keys = jnp.concatenate([keys, fresh[at, :HEAD_WIDTH], pad], axis=0)
                values = jnp.concatenate([values, fresh[at, HEAD_WIDTH:], pad], axis=0)
                values = jnp.concatenate([values, ones], axis=1)
                ends = jnp.zeros(spot.shape, jnp.int32)
                for i in range(half):
                    ends = jnp.where(owner == i, lengths[seg * 2 * half + h * half + i], ends)
                bias = jnp.concatenate([jnp.where(nth < ends, 0.0, -jnp.inf), no_bias], axis=1)
                scores = lax.dot_general(
                    q, keys, (((1,), (1,)), ((), ())), preferred_element_type=jnp.float32
                )
                scores = scores + (same[...] + bias)
                lifted = jnp.exp2((scores - jnp.max(scores, axis=1, keepdims=True)) * unit)
                mixed = jnp.dot(lifted.astype(jnp.bfloat16), values, preferred_element_type=jnp.float32)
                mixed = mixed[:, :HEAD_WIDTH] / mixed[:, HEAD_WIDTH:]
                out = jnp.concatenate(
                    [mixed[g * rows : (g + 1) * rows] for g in range(heads)], axis=1
                )
                place = h * half + lax.broadcasted_iota(jnp.int32, out.shape, 0) // 2
                outs.append(jnp.where(place < live[seg], out, 0.0).astype(jnp.bfloat16))
            return jnp.concatenate(outs, axis=0).reshape((per_seg,) + out_ref.shape[1:])

        def pair(i, _):
            outs = [segment(2 * i + k) for k in range(2)]
            for k in range(2):
                out_ref[pl.ds((2 * i + k) * per_seg, per_seg)] = outs[k]
            return 0

        lax.fori_loop(0, x_ref.shape[0] // 2, pair, 0)

    def returned(chunk):
        def wait(j, _):
            d_copy(chunk, j).wait_recv()
            return 0

        lax.fori_loop(1 if chunk == 0 else 0, PER, wait, 0)

    weight_z(4, 3, 5, 2, 6, 1, 7)
    send_inputs(0)
    send_inputs(1)
    prepare()
    loads[1].wait()
    shrink_parts(0)
    weight_first(0)
    send_inputs(2)
    send_inputs(3)
    loads[2].wait()
    loads[3].wait()
    weight_second(0)
    weight_first(1)
    add_up(0)
    weight_third(0)
    ring(0)
    shrink_parts(1)
    weight_second(1)
    weight_first(2)
    give_back(0)
    weight_third(1)
    ring(1)
    add_up(1)
    shrink_parts(2)
    weight_second(2)
    weight_first(3)
    weight_first(4)
    shrink_parts(3)
    add_up(2)
    give_back(1)
    weight_third(2)
    ring(2)
    weight_second(3)
    weight_second(4)
    add_up(3)
    give_back(2)
    weight_third(3)
    ring(3)
    give_back(3)
    weight_third(4)
    ring_end()
    loads[4].wait()
    for chunk in range(CHUNKS):
        returned(chunk)
    attend()

    for chunk in range(CHUNKS):
        def settle(j, _, chunk=chunk):
            x_copy(chunk, j).wait_send()
            d_copy(chunk, j).wait_send()
            return 0

        lax.fori_loop(1 if chunk == 0 else 0, PER, settle, 0)

        def settle_z(i, _, chunk=chunk):
            rs_copy(chunk, (t + i) % TZ, t).wait_send()
            ag_copy(chunk, (t + i) % TZ, t).wait_send()
            return 0

        lax.fori_loop(1, TZ, settle_z, 0)

    def settle_w(i, _):
        wz_copy((t + i) % TZ, t).wait_send()
        return 0

    lax.fori_loop(1, TZ, settle_w, 0)
    def settle_shares(u, _):
        wp_copy(u).wait_send()
        ws_copy(u, 0).wait_send()
        ws_copy(u, 1).wait_send()
        return 0

    lax.fori_loop(0, TZ, settle_shares, 0)

    for s in range(4):
        for i in range(tiles):
            if s >= i:
                right_copy(s, i).wait_send()
            if s >= 1 - i:
                left_copy(s, i).wait_send()


def layer(tables, x, down, upq, upkv, q, cache, weight):
    segs = tables[1].shape[0]
    tokens, features = x.shape[1:]
    per_seg = x.shape[0] // segs
    rows = per_seg * tokens
    packed_rows = rows * down.shape[1] // HEAD_WIDTH
    kv = weight.shape[1] * weight.shape[2]
    wide = q.shape[2]
    columns = wide + kv
    smem = pl.BlockSpec(memory_space=pltpu.SMEM)
    vmem = pl.BlockSpec(memory_space=pltpu.VMEM)
    hbm = pl.BlockSpec(memory_space=pltpu.HBM)
    dma = pltpu.SemaphoreType.DMA
    tiles = segs * rows // 256
    half_rows = rows // 2 * (wide // HEAD_WIDTH)
    loaded = [x, down, upq, upkv, q, cache]

    def room(*shape, dtype=jnp.bfloat16):
        return pltpu.VMEM(shape, dtype)

    return pl.pallas_call(
        layer_kernel,
        out_shape=jax.ShapeDtypeStruct(q.shape, jnp.bfloat16),
        in_specs=[smem] * len(tables) + [hbm] * (len(loaded) + 1),
        out_specs=vmem,
        scratch_shapes=[room(*a.shape) for a in loaded]
        + [
            dma((len(loaded),)),
            room(segs, rows, features),
            room(segs, rows, wide),
            room(segs, rows, kv, dtype=jnp.float32),
            room(half_rows, rows // 4 * CTX + 128, dtype=jnp.float32),
            room(SLOTS, rows, features),
            room(SLOTS, rows, features),
            room(SLOTS, packed_rows, HEAD_WIDTH),
            room(CHUNKS, TZ, packed_rows, HEAD_WIDTH),
            room(CHUNKS, TZ, packed_rows, HEAD_WIDTH),
            room(SLOTS, rows, columns),
            room(SLOTS, rows, columns),
            room(TZ, 2, 2, features // 4, *weight.shape[1:]),
            room(4, segs * rows, kv),
            room(4, segs * rows, kv),
            room(4, segs * rows, kv),
            room(4, segs * rows, kv),
            room(2, features, kv),
            dma((SLOTS,)), dma((SLOTS,)),
            dma((CHUNKS, TZ)), dma((CHUNKS, TZ)), dma((CHUNKS, TZ)), dma((CHUNKS, TZ)),
            dma((SLOTS,)), dma((SLOTS,)),
            dma((TZ,)), dma((TZ,)),
            dma((TZ,)), dma((TZ,)), dma((TZ, 2)), dma((TZ, 2)), dma((1,)),
            dma((4, tiles)), dma((4, tiles)), dma((4, tiles)), dma((4, tiles)),
        ],
        compiler_params=pltpu.CompilerParams(
            collective_id=0, has_side_effects=True, vmem_limit_bytes=52 * 2**20
        ),
        name="layer",
    )(*tables, *loaded, weight)


def shards(
    normed_token_input,
    rotated_base_query,
    key_value_weight,
    key_value_cache,
    adapter_down_maps,
    query_up_maps,
    key_value_up_maps,
    adapter_storage_row,
    segment_adapter,
    segment_live_requests,
    cache_length,
):
    requests, tokens, features = normed_token_input.shape
    wide = rotated_base_query.shape[2]
    kv_wide = key_value_weight.shape[2]
    owned = adapter_down_maps.shape[0]
    replicas = lax.axis_size("replica")
    segs = segment_live_requests.shape[0]
    me = lax.axis_index("replica")

    adapter_ids = jnp.arange(adapter_storage_row.shape[0], dtype=jnp.int32)
    slot = jnp.sum(
        jnp.where(
            segment_adapter[:, None] == adapter_ids[None, :], adapter_storage_row[None, :], 0
        ),
        axis=1,
    ).reshape(replicas, segs)
    group, local = lax.div(slot, owned), lax.rem(slot, owned)
    group_of_seg = lax.dynamic_index_in_dim(group, me, 0, keepdims=False)
    group_ids = jnp.arange(replicas, dtype=jnp.int32)
    seg_ids = jnp.arange(segs, dtype=jnp.int32)
    seg_of_group = jnp.sum(
        jnp.where(group_of_seg[None, :] == group_ids[:, None], seg_ids[None, :], 0), axis=1
    )
    local_of_replica = jnp.sum(jnp.where(group == me, local, 0), axis=1)

    return layer(
        (seg_of_group, group_of_seg, local_of_replica, segment_live_requests, cache_length),
        normed_token_input, adapter_down_maps, query_up_maps, key_value_up_maps,
        rotated_base_query,
        key_value_cache.reshape((segs, requests // segs) + key_value_cache.shape[1:]),
        key_value_weight,
    )


def solution(mesh):
    return jax.shard_map(
        shards,
        mesh=mesh,
        in_specs=(
            P("replica", None, "tensor"),
            P("replica", None, "tensor"),
            P(None, None, "tensor"),
            P("replica", None, None, "tensor"),
            P("replica", None, "tensor"),
            P("replica", None, "tensor"),
            P("replica", None, None, "tensor"),
            P(),
            P(),
            P("replica"),
            P("replica"),
        ),
        out_specs=P("replica", None, "tensor"),
        check_vma=False,
    )
```

```python
import functools
import math

import jax
import jax.numpy as jnp
from jax import lax
from jax.experimental import pallas as pl
from jax.experimental.pallas import tpu as pltpu
from jax.sharding import PartitionSpec as P

HEAD_WIDTH = 128
CTX = 32
ADAPTER_SCALE = 0.5
MESH = pl.DeviceIdType.MESH

RINGS = (
    ((2, 2),),
    ((2, 1), (1, 2), (2, 3), (3, 2)),
    ((0, 2), (2, 0)),
    ((1, 1), (3, 3), (1, 3), (3, 1)),
    ((0, 1), (1, 0), (0, 3), (3, 0)),
)
OFFSETS = [(0, 0, 0)] + [(dy, dx, dc) for ring in RINGS for dc in (0, 1) for dy, dx in ring] + [(0, 0, 1)]
SLOTS = 32
CHUNKS = 4
PER = SLOTS // CHUNKS
TZ = 8


def packed(chunk, which, bits):
    total = 0
    for j in range(PER):
        total += OFFSETS[chunk * PER + j][which] << (bits * j)
    return total


PACK_Y = [packed(c, 0, 2) for c in range(CHUNKS)]
PACK_X = [packed(c, 1, 2) for c in range(CHUNKS)]
PACK_C = [packed(c, 2, 1) for c in range(CHUNKS)]


def offset(chunk, j):
    return (
        (PACK_Y[chunk] >> (2 * j)) & 3,
        (PACK_X[chunk] >> (2 * j)) & 3,
        (PACK_C[chunk] >> j) & 1,
    )


def moved(me, off, sign):
    y, x, c = me // 8, (me // 2) % 4, me % 2
    dy, dx, dc = off
    return ((y + 4 + sign * dy) % 4) * 8 + ((x + 4 + sign * dx) % 4) * 2 + (c + dc) % 2


def layer_kernel(
    seg_of_group, group_of_seg, local_of_replica, live, lengths,
    x_hbm, down_hbm, upq_hbm, upkv_hbm, q_hbm, cache_hbm, w_hbm,
    out_ref,
    x_raw, down_ref, upq_ref, upkv_ref, q_raw, cache_ref, load_sem,
    x_ref, q_ref, base_ref, same,
    xs, xr, part, rs, ag, ds, dr, wall, right_out, right_in, left_out, left_in, wnow,
    x_send, x_recv, rs_send, rs_recv, ag_send, ag_recv, d_send, d_recv,
    wz_send, wz_recv, wp_send, wp_recv, ws_send, ws_recv, own_sem,
    right_send, right_recv, left_send, left_recv,
):
    me = lax.axis_index("replica")
    t = lax.axis_index("tensor")
    y, x, core = me // 8, (me // 2) % 4, me % 2

    barrier = pltpu.get_barrier_semaphore()

    def greet_plane(i, _):
        pl.semaphore_signal(barrier, inc=1, device_id=((me + i) % SLOTS, t), device_id_type=MESH)
        return 0

    def greet_z(i, _):
        pl.semaphore_signal(barrier, inc=1, device_id=(me, (t + i) % TZ), device_id_type=MESH)
        return 0

    lax.fori_loop(1, SLOTS, greet_plane, 0)
    lax.fori_loop(1, TZ, greet_z, 0)

    loads = [
        pltpu.make_async_copy(src, dst, load_sem.at[i])
        for i, (src, dst) in enumerate(
            [(x_hbm, x_raw), (down_hbm, down_ref), (upq_hbm, upq_ref), (upkv_hbm, upkv_ref),
             (cache_hbm, cache_ref), (q_hbm, q_raw)]
        )
    ]
    for load in loads:
        load.start()

    def x_copy(chunk, j):
        p = chunk * PER + j
        return pltpu.make_async_remote_copy(
            src_ref=xs.at[p], dst_ref=xr.at[p], send_sem=x_send.at[p], recv_sem=x_recv.at[p],
            device_id=(moved(me, offset(chunk, j), 1), t), device_id_type=MESH,
        )

    def d_copy(chunk, j):
        p = chunk * PER + j
        return pltpu.make_async_remote_copy(
            src_ref=ds.at[p], dst_ref=dr.at[me], send_sem=d_send.at[p], recv_sem=d_recv.at[p],
            device_id=(moved(me, offset(chunk, j), -1), t), device_id_type=MESH,
        )

    def rs_copy(chunk, u, sender):
        return pltpu.make_async_remote_copy(
            src_ref=part.at[chunk * PER + u], dst_ref=rs.at[chunk, sender],
            send_sem=rs_send.at[chunk, u], recv_sem=rs_recv.at[chunk, sender],
            device_id=(me, u), device_id_type=MESH,
        )

    def ag_copy(chunk, u, sender):
        return pltpu.make_async_remote_copy(
            src_ref=ag.at[chunk, sender], dst_ref=ag.at[chunk, sender],
            send_sem=ag_send.at[chunk, u], recv_sem=ag_recv.at[chunk, sender],
            device_id=(me, u), device_id_type=MESH,
        )

    def pair_of(share):
        quarter = share // 2
        on_y = quarter // 2
        b = (jnp.where(on_y == 1, y, x) + quarter % 2) % 2
        step = 1 + 2 * b
        partner = jnp.where(
            on_y == 1, ((y + step) % 4) * 8 + x * 2 + core, y * 8 + ((x + step) % 4) * 2 + core
        )
        return b, partner

    def own_rows(u):
        place = core * 2 + pair_of(t)[0]
        return w_hbm.at[pl.ds((u * 4 + place) * wall.shape[3], wall.shape[3])]

    def wz_copy(u, sender):
        return pltpu.make_async_remote_copy(
            src_ref=own_rows(u), dst_ref=wall.at[sender, core, pair_of(sender)[0]],
            send_sem=wz_send.at[u], recv_sem=wz_recv.at[sender],
            device_id=(me, u), device_id_type=MESH,
        )

    def wp_copy(u):
        b, partner = pair_of(u)
        piece = wall.at[u, core, b]
        return pltpu.make_async_remote_copy(
            src_ref=piece, dst_ref=piece, send_sem=wp_send.at[u], recv_sem=wp_recv.at[u],
            device_id=(partner, t), device_id_type=MESH,
        )

    def ws_copy(u, k):
        b = pair_of(u)[0]
        piece = wall.at[u, core, (b + k) % 2]
        return pltpu.make_async_remote_copy(
            src_ref=piece, dst_ref=piece, send_sem=ws_send.at[u, k], recv_sem=ws_recv.at[u, k],
            device_id=(y * 8 + x * 2 + 1 - core, t), device_id_type=MESH,
        )

    own_weight = pltpu.make_async_copy(
        own_rows(t), wall.at[t, core, pair_of(t)[0]], own_sem.at[0]
    )

    def weight_z(*hops):
        for d in hops:
            wz_copy((t + d) % TZ, t).start()

    steps = ((4,), (3, 5), (2, 6), (1, 7), (0,))

    def weight_first(s):
        for d in steps[s]:
            u = (t + d) % TZ
            if d:
                wz_copy(t, u).wait_recv()
            else:
                own_weight.wait()
            wp_copy(u).start()
            ws_copy(u, 0).start()

    def weight_second(s):
        for d in steps[s]:
            u = (t + d) % TZ
            wp_copy(u).wait_recv()
            ws_copy(u, 1).start()

    def weight_third(s):
        for d in steps[s]:
            u = (t + d) % TZ
            ws_copy(u, 0).wait_recv()
            ws_copy(u, 1).wait_recv()

    tall = 256
    segs_of_tile = tall // x_ref.shape[1]
    tiles = x_ref.shape[0] // segs_of_tile

    def right_copy(s, i):
        at = pl.ds(i * tall, tall)
        return pltpu.make_async_remote_copy(
            src_ref=right_out.at[s, at], dst_ref=right_in.at[s, at],
            send_sem=right_send.at[s, i], recv_sem=right_recv.at[s, i],
            device_id=(me, (t + 1) % TZ), device_id_type=MESH,
        )

    def left_copy(s, i):
        at = pl.ds(i * tall, tall)
        return pltpu.make_async_remote_copy(
            src_ref=left_out.at[s, at], dst_ref=left_in.at[s, at],
            send_sem=left_send.at[s, i], recv_sem=left_recv.at[s, i],
            device_id=(me, (t + TZ - 1) % TZ), device_id_type=MESH,
        )

    def weight_of(share, k):
        wide_rows = wall[share].reshape((x_ref.shape[2],) + wall.shape[4:])
        wnow[k] = wide_rows.reshape(wnow.shape[1:])

    def base_part(k, i):
        rows = x_ref[pl.ds(i * segs_of_tile, segs_of_tile)].reshape(tall, x_ref.shape[2])
        return jnp.dot(rows, wnow[k], preferred_element_type=jnp.float32)

    def pass_right(s, i, value):
        at = pl.ds(i * tall, tall)
        if s > i:
            right_copy(s - 1, i).wait_recv()
            value = value + right_in[s - 1, at].astype(jnp.float32)
        right_out[s, at] = value.astype(jnp.bfloat16)
        right_copy(s, i).start()

    def pass_left(s, i, value):
        at = pl.ds(i * tall, tall)
        if s > 1 - i:
            left_copy(s - 1, i).wait_recv()
            value = value + left_in[s - 1, at].astype(jnp.float32)
        left_out[s, at] = value.astype(jnp.bfloat16)
        left_copy(s, i).start()

    def ring(s):
        for k, d in enumerate(steps[s]):
            weight_of((t + d) % TZ, k)
        if s == 0:
            pass_right(0, 0, base_part(0, 0))
            pass_left(0, 1, base_part(0, 1))
        else:
            for i in range(tiles):
                pass_right(s, i, base_part(0, i))
                pass_left(s, i, base_part(1, i))

    def ring_end():
        weight_of(t, 0)
        for i in range(tiles):
            at = pl.ds(i * tall, tall)
            value = base_part(0, i)
            left_copy(3, i).wait_recv()
            right_copy(3, i).wait_recv()
            value = value + right_in[3, at].astype(jnp.float32) + left_in[3, at].astype(jnp.float32)
            base_ref[pl.ds(i * segs_of_tile, segs_of_tile)] = value.reshape(
                segs_of_tile, base_ref.shape[1], base_ref.shape[2]
            )

    per_seg = x_raw.shape[0] // x_ref.shape[0]

    def by_rows(raw, ref):
        def one(s, _):
            ref[s] = raw[pl.ds(s * per_seg, per_seg)].reshape(ref.shape[1:])
            return 0

        lax.fori_loop(0, ref.shape[0], one, 0)

    loads[0].wait()
    by_rows(x_raw, x_ref)
    for chunk in range(CHUNKS):
        def fill(j, _, chunk=chunk):
            group = moved(me, offset(chunk, j), 1)
            xs[chunk * PER + j] = x_ref[seg_of_group[group]]
            return 0

        lax.fori_loop(0, PER, fill, 0)
    pl.semaphore_wait(barrier, SLOTS - 1 + TZ - 1)
    own_weight.start()

    def send_inputs(chunk):
        def send(j, _):
            x_copy(chunk, j).start()
            return 0

        lax.fori_loop(1 if chunk == 0 else 0, PER, send, 0)

    def packed_shrink(shrink):
        mid = shrink.shape[0] // 2
        value = jnp.concatenate([shrink[:mid, 128:], shrink[mid:, 128:]], axis=1)
        return jnp.concatenate([shrink[:, :128], value], axis=0)

    def shrink_parts(chunk):
        def one(j, _):
            p = chunk * PER + j
            rows = xs[0] if chunk == 0 and isinstance(j, int) else xr[p]
            w = down_ref[local_of_replica[moved(me, offset(chunk, j), -1)]]
            shrink = lax.dot_general(
                rows, w, (((1,), (1,)), ((), ())), preferred_element_type=jnp.float32
            )
            part[p] = packed_shrink(shrink).astype(jnp.bfloat16)
            return 0

        def arrived(j, _):
            x_copy(chunk, j).wait_recv()
            return one(j, 0)

        if chunk == 0:
            one(0, 0)
        lax.fori_loop(1 if chunk == 0 else 0, PER, arrived, 0)

        def send(i, _):
            rs_copy(chunk, (t + i) % TZ, t).start()
            return 0

        lax.fori_loop(1, TZ, send, 0)

    def add_up(chunk):
        def wait(i, _):
            rs_copy(chunk, t, (t + TZ - i) % TZ).wait_recv()
            return 0

        lax.fori_loop(1, TZ, wait, 0)
        rs[chunk, t] = part[chunk * PER + t]
        total = rs[chunk, 0].astype(jnp.float32)
        for u in range(1, TZ):
            total = total + rs[chunk, u].astype(jnp.float32)
        ag[chunk, t] = total.astype(jnp.bfloat16)

        def send(i, _):
            ag_copy(chunk, (t + i) % TZ, t).start()
            return 0

        lax.fori_loop(1, TZ, send, 0)

    def give_back(chunk):
        def wait(i, _):
            ag_copy(chunk, t, (t + TZ - i) % TZ).wait_recv()
            return 0

        lax.fori_loop(1, TZ, wait, 0)

        def deltas(j):
            a = local_of_replica[moved(me, offset(chunk, j), -1)]
            both = ag[chunk, j]
            mid = both.shape[0] // 3
            shrink, value = both[: 2 * mid], both[2 * mid :]
            value = jnp.concatenate([value[:, :64], value[:, 64:]], axis=0)
            q = jnp.dot(shrink[:, 0:64], upq_ref[a], preferred_element_type=jnp.float32)
            k = jnp.dot(shrink[:, 64:128], upkv_ref[a, 0], preferred_element_type=jnp.float32)
            v = jnp.dot(value, upkv_ref[a, 1], preferred_element_type=jnp.float32)
            return jnp.concatenate([q, k, v], axis=1).astype(jnp.bfloat16)

        def one(j, _):
            ds[chunk * PER + j] = deltas(j)
            d_copy(chunk, j).start()
            return 0

        if chunk == 0:
            dr[me] = deltas(0)
        lax.fori_loop(1 if chunk == 0 else 0, PER, one, 0)

    half = 8
    heads = q_ref.shape[2] // HEAD_WIDTH
    wide = q_ref.shape[2]
    rows = half * 2
    n = heads * rows
    unit = math.log2(math.e) / math.sqrt(HEAD_WIDTH)

    old_keys = half * CTX
    all_keys = same.shape[1]

    def prepare():
        row = lax.broadcasted_iota(jnp.int32, same.shape, 0) % rows
        col = lax.broadcasted_iota(jnp.int32, same.shape, 1)
        new = col - old_keys
        old_fits = jnp.where(row // 2 == col // CTX, 0.0, -jnp.inf)
        new_fits = jnp.where((row // 2 == new // 2) & (new <= row), 0.0, -jnp.inf)
        same[...] = jnp.where(new < 0, old_fits, new_fits)
        loads[5].wait()
        by_rows(q_raw, q_ref)

    def attend():
        spot = lax.broadcasted_iota(jnp.int32, (1, old_keys), 1)
        owner, nth = spot // CTX, spot % CTX
        pad = jnp.zeros((all_keys - old_keys - rows, HEAD_WIDTH), jnp.bfloat16)
        ones = jnp.ones((all_keys, HEAD_WIDTH), jnp.bfloat16)
        no_bias = jnp.zeros((1, all_keys - old_keys), jnp.float32)

        def segment(seg):
            delta = dr[group_of_seg[seg]].astype(jnp.float32) * ADAPTER_SCALE
            q_all = (q_ref[seg].astype(jnp.float32) + delta[:, :wide]).astype(jnp.bfloat16)
            fresh = (base_ref[seg] + delta[:, wide:]).astype(jnp.bfloat16)
            outs = []
            for h in range(2):
                at = slice(h * rows, (h + 1) * rows)
                q = jnp.concatenate(
                    [q_all[at, g * HEAD_WIDTH : (g + 1) * HEAD_WIDTH] for g in range(heads)], axis=0
                )
                keys = cache_ref[seg, h * half : (h + 1) * half, 0].reshape(old_keys, HEAD_WIDTH)
                values = cache_ref[seg, h * half : (h + 1) * half, 1].reshape(old_keys, HEAD_WIDTH)
                keys = jnp.concatenate([keys, fresh[at, :HEAD_WIDTH], pad], axis=0)
                values = jnp.concatenate([values, fresh[at, HEAD_WIDTH:], pad], axis=0)
                values = jnp.concatenate([values, ones], axis=1)
                ends = jnp.zeros(spot.shape, jnp.int32)
                for i in range(half):
                    ends = jnp.where(owner == i, lengths[seg * 2 * half + h * half + i], ends)
                bias = jnp.concatenate([jnp.where(nth < ends, 0.0, -jnp.inf), no_bias], axis=1)
                scores = lax.dot_general(
                    q, keys, (((1,), (1,)), ((), ())), preferred_element_type=jnp.float32
                )
                scores = scores + (same[...] + bias)
                lifted = jnp.exp2((scores - jnp.max(scores, axis=1, keepdims=True)) * unit)
                mixed = jnp.dot(lifted.astype(jnp.bfloat16), values, preferred_element_type=jnp.float32)
                mixed = mixed[:, :HEAD_WIDTH] / mixed[:, HEAD_WIDTH:]
                out = jnp.concatenate(
                    [mixed[g * rows : (g + 1) * rows] for g in range(heads)], axis=1
                )
                place = h * half + lax.broadcasted_iota(jnp.int32, out.shape, 0) // 2
                outs.append(jnp.where(place < live[seg], out, 0.0).astype(jnp.bfloat16))
            return jnp.concatenate(outs, axis=0).reshape((per_seg,) + out_ref.shape[1:])

        def pair(i, _):
            outs = [segment(2 * i + k) for k in range(2)]
            for k in range(2):
                out_ref[pl.ds((2 * i + k) * per_seg, per_seg)] = outs[k]
            return 0

        lax.fori_loop(0, x_ref.shape[0] // 2, pair, 0)

    def returned(chunk):
        def wait(j, _):
            d_copy(chunk, j).wait_recv()
            return 0

        lax.fori_loop(1 if chunk == 0 else 0, PER, wait, 0)

    weight_z(4, 3, 5)
    send_inputs(0)
    send_inputs(1)
    prepare()
    loads[1].wait()
    shrink_parts(0)
    weight_z(2, 6, 1, 7)
    weight_first(0)
    send_inputs(2)
    send_inputs(3)
    loads[2].wait()
    loads[3].wait()
    weight_second(0)
    weight_first(1)
    add_up(0)
    weight_third(0)
    ring(0)
    shrink_parts(1)
    weight_second(1)
    weight_first(2)
    give_back(0)
    weight_third(1)
    ring(1)
    add_up(1)
    shrink_parts(2)
    weight_second(2)
    weight_first(3)
    weight_first(4)
    shrink_parts(3)
    add_up(2)
    give_back(1)
    weight_third(2)
    ring(2)
    weight_second(3)
    weight_second(4)
    add_up(3)
    give_back(2)
    weight_third(3)
    ring(3)
    give_back(3)
    weight_third(4)
    ring_end()
    loads[4].wait()
    for chunk in range(CHUNKS):
        returned(chunk)
    attend()

    for chunk in range(CHUNKS):
        def settle(j, _, chunk=chunk):
            x_copy(chunk, j).wait_send()
            d_copy(chunk, j).wait_send()
            return 0

        lax.fori_loop(1 if chunk == 0 else 0, PER, settle, 0)

        def settle_z(i, _, chunk=chunk):
            rs_copy(chunk, (t + i) % TZ, t).wait_send()
            ag_copy(chunk, (t + i) % TZ, t).wait_send()
            return 0

        lax.fori_loop(1, TZ, settle_z, 0)

    def settle_w(i, _):
        wz_copy((t + i) % TZ, t).wait_send()
        return 0

    lax.fori_loop(1, TZ, settle_w, 0)
    def settle_shares(u, _):
        wp_copy(u).wait_send()
        ws_copy(u, 0).wait_send()
        ws_copy(u, 1).wait_send()
        return 0

    lax.fori_loop(0, TZ, settle_shares, 0)

    for s in range(4):
        for i in range(tiles):
            if s >= i:
                right_copy(s, i).wait_send()
            if s >= 1 - i:
                left_copy(s, i).wait_send()


def layer(tables, x, down, upq, upkv, q, cache, weight):
    segs = tables[1].shape[0]
    tokens, features = x.shape[1:]
    per_seg = x.shape[0] // segs
    rows = per_seg * tokens
    packed_rows = rows * down.shape[1] // HEAD_WIDTH
    kv = weight.shape[1] * weight.shape[2]
    wide = q.shape[2]
    columns = wide + kv
    smem = pl.BlockSpec(memory_space=pltpu.SMEM)
    vmem = pl.BlockSpec(memory_space=pltpu.VMEM)
    hbm = pl.BlockSpec(memory_space=pltpu.HBM)
    dma = pltpu.SemaphoreType.DMA
    tiles = segs * rows // 256
    half_rows = rows // 2 * (wide // HEAD_WIDTH)
    loaded = [x, down, upq, upkv, q, cache]

    def room(*shape, dtype=jnp.bfloat16):
        return pltpu.VMEM(shape, dtype)

    return pl.pallas_call(
        layer_kernel,
        out_shape=jax.ShapeDtypeStruct(q.shape, jnp.bfloat16),
        in_specs=[smem] * len(tables) + [hbm] * (len(loaded) + 1),
        out_specs=vmem,
        scratch_shapes=[room(*a.shape) for a in loaded]
        + [
            dma((len(loaded),)),
            room(segs, rows, features),
            room(segs, rows, wide),
            room(segs, rows, kv, dtype=jnp.float32),
            room(half_rows, rows // 4 * CTX + 128, dtype=jnp.float32),
            room(SLOTS, rows, features),
            room(SLOTS, rows, features),
            room(SLOTS, packed_rows, HEAD_WIDTH),
            room(CHUNKS, TZ, packed_rows, HEAD_WIDTH),
            room(CHUNKS, TZ, packed_rows, HEAD_WIDTH),
            room(SLOTS, rows, columns),
            room(SLOTS, rows, columns),
            room(TZ, 2, 2, features // 4, *weight.shape[1:]),
            room(4, segs * rows, kv),
            room(4, segs * rows, kv),
            room(4, segs * rows, kv),
            room(4, segs * rows, kv),
            room(2, features, kv),
            dma((SLOTS,)), dma((SLOTS,)),
            dma((CHUNKS, TZ)), dma((CHUNKS, TZ)), dma((CHUNKS, TZ)), dma((CHUNKS, TZ)),
            dma((SLOTS,)), dma((SLOTS,)),
            dma((TZ,)), dma((TZ,)),
            dma((TZ,)), dma((TZ,)), dma((TZ, 2)), dma((TZ, 2)), dma((1,)),
            dma((4, tiles)), dma((4, tiles)), dma((4, tiles)), dma((4, tiles)),
        ],
        compiler_params=pltpu.CompilerParams(
            collective_id=0, has_side_effects=True, vmem_limit_bytes=52 * 2**20
        ),
        name="layer",
    )(*tables, *loaded, weight)


def shards(
    normed_token_input,
    rotated_base_query,
    key_value_weight,
    key_value_cache,
    adapter_down_maps,
    query_up_maps,
    key_value_up_maps,
    adapter_storage_row,
    segment_adapter,
    segment_live_requests,
    cache_length,
):
    requests, tokens, features = normed_token_input.shape
    wide = rotated_base_query.shape[2]
    kv_wide = key_value_weight.shape[2]
    owned = adapter_down_maps.shape[0]
    replicas = lax.axis_size("replica")
    segs = segment_live_requests.shape[0]
    me = lax.axis_index("replica")

    adapter_ids = jnp.arange(adapter_storage_row.shape[0], dtype=jnp.int32)
    slot = jnp.sum(
        jnp.where(
            segment_adapter[:, None] == adapter_ids[None, :], adapter_storage_row[None, :], 0
        ),
        axis=1,
    ).reshape(replicas, segs)
    group, local = lax.div(slot, owned), lax.rem(slot, owned)
    group_of_seg = lax.dynamic_index_in_dim(group, me, 0, keepdims=False)
    group_ids = jnp.arange(replicas, dtype=jnp.int32)
    seg_ids = jnp.arange(segs, dtype=jnp.int32)
    seg_of_group = jnp.sum(
        jnp.where(group_of_seg[None, :] == group_ids[:, None], seg_ids[None, :], 0), axis=1
    )
    local_of_replica = jnp.sum(jnp.where(group == me, local, 0), axis=1)

    return layer(
        (seg_of_group, group_of_seg, local_of_replica, segment_live_requests, cache_length),
        normed_token_input, adapter_down_maps, query_up_maps, key_value_up_maps,
        rotated_base_query,
        key_value_cache.reshape((segs, requests // segs) + key_value_cache.shape[1:]),
        key_value_weight,
    )


def solution(mesh):
    return jax.shard_map(
        shards,
        mesh=mesh,
        in_specs=(
            P("replica", None, "tensor"),
            P("replica", None, "tensor"),
            P(None, None, "tensor"),
            P("replica", None, None, "tensor"),
            P("replica", None, "tensor"),
            P("replica", None, "tensor"),
            P("replica", None, None, "tensor"),
            P(),
            P(),
            P("replica"),
            P("replica"),
        ),
        out_specs=P("replica", None, "tensor"),
        check_vma=False,
    )
```

```python
import functools
import math

import jax
import jax.numpy as jnp
from jax import lax
from jax.experimental import pallas as pl
from jax.experimental.pallas import tpu as pltpu
from jax.sharding import PartitionSpec as P

HEAD_WIDTH = 128
CTX = 32
ADAPTER_SCALE = 0.5
MESH = pl.DeviceIdType.MESH

RINGS = (
    ((2, 2),),
    ((2, 1), (1, 2), (2, 3), (3, 2)),
    ((0, 2), (2, 0)),
    ((1, 1), (3, 3), (1, 3), (3, 1)),
    ((0, 1), (1, 0), (0, 3), (3, 0)),
)
OFFSETS = [(0, 0, 0)] + [(dy, dx, dc) for ring in RINGS for dc in (0, 1) for dy, dx in ring] + [(0, 0, 1)]
SLOTS = 32
CHUNKS = 4
PER = SLOTS // CHUNKS
TZ = 8


def packed(chunk, which, bits):
    total = 0
    for j in range(PER):
        total += OFFSETS[chunk * PER + j][which] << (bits * j)
    return total


PACK_Y = [packed(c, 0, 2) for c in range(CHUNKS)]
PACK_X = [packed(c, 1, 2) for c in range(CHUNKS)]
PACK_C = [packed(c, 2, 1) for c in range(CHUNKS)]


def offset(chunk, j):
    return (
        (PACK_Y[chunk] >> (2 * j)) & 3,
        (PACK_X[chunk] >> (2 * j)) & 3,
        (PACK_C[chunk] >> j) & 1,
    )


def moved(me, off, sign):
    y, x, c = me // 8, (me // 2) % 4, me % 2
    dy, dx, dc = off
    return ((y + 4 + sign * dy) % 4) * 8 + ((x + 4 + sign * dx) % 4) * 2 + (c + dc) % 2


def layer_kernel(
    seg_of_group, group_of_seg, local_of_replica, live, lengths,
    x_hbm, down_hbm, upq_hbm, upkv_hbm, q_hbm, cache_hbm, w_hbm,
    out_ref,
    x_raw, down_ref, upq_ref, upkv_ref, q_raw, cache_ref, load_sem,
    x_ref, q_ref, base_ref, same,
    xs, xr, part, rs, ag, ds, dr, wall, right_out, right_in, left_out, left_in, wnow,
    x_send, x_recv, rs_send, rs_recv, ag_send, ag_recv, d_send, d_recv,
    wz_send, wz_recv, wp_send, wp_recv, ws_send, ws_recv, own_sem,
    right_send, right_recv, left_send, left_recv,
):
    me = lax.axis_index("replica")
    t = lax.axis_index("tensor")
    y, x, core = me // 8, (me // 2) % 4, me % 2

    barrier = pltpu.get_barrier_semaphore()

    def greet_plane(i, _):
        pl.semaphore_signal(barrier, inc=1, device_id=((me + i) % SLOTS, t), device_id_type=MESH)
        return 0

    def greet_z(i, _):
        pl.semaphore_signal(barrier, inc=1, device_id=(me, (t + i) % TZ), device_id_type=MESH)
        return 0

    lax.fori_loop(1, SLOTS, greet_plane, 0)
    lax.fori_loop(1, TZ, greet_z, 0)

    loads = [
        pltpu.make_async_copy(src, dst, load_sem.at[i])
        for i, (src, dst) in enumerate(
            [(x_hbm, x_raw), (down_hbm, down_ref), (upq_hbm, upq_ref), (upkv_hbm, upkv_ref),
             (cache_hbm, cache_ref), (q_hbm, q_raw)]
        )
    ]
    for load in loads:
        load.start()

    def x_copy(chunk, j):
        p = chunk * PER + j
        return pltpu.make_async_remote_copy(
            src_ref=xs.at[p], dst_ref=xr.at[p], send_sem=x_send.at[p], recv_sem=x_recv.at[p],
            device_id=(moved(me, offset(chunk, j), 1), t), device_id_type=MESH,
        )

    def d_copy(chunk, j):
        p = chunk * PER + j
        return pltpu.make_async_remote_copy(
            src_ref=ds.at[p], dst_ref=dr.at[me], send_sem=d_send.at[p], recv_sem=d_recv.at[p],
            device_id=(moved(me, offset(chunk, j), -1), t), device_id_type=MESH,
        )

    def rs_copy(chunk, u, sender):
        return pltpu.make_async_remote_copy(
            src_ref=part.at[chunk * PER + u], dst_ref=rs.at[chunk, sender],
            send_sem=rs_send.at[chunk, u], recv_sem=rs_recv.at[chunk, sender],
            device_id=(me, u), device_id_type=MESH,
        )

    def ag_copy(chunk, u, sender):
        return pltpu.make_async_remote_copy(
            src_ref=ag.at[chunk, sender], dst_ref=ag.at[chunk, sender],
            send_sem=ag_send.at[chunk, u], recv_sem=ag_recv.at[chunk, sender],
            device_id=(me, u), device_id_type=MESH,
        )

    def pair_of(share):
        quarter = share // 2
        on_y = quarter // 2
        b = (jnp.where(on_y == 1, y, x) + quarter % 2) % 2
        step = 1 + 2 * b
        partner = jnp.where(
            on_y == 1, ((y + step) % 4) * 8 + x * 2 + core, y * 8 + ((x + step) % 4) * 2 + core
        )
        return b, partner

    def own_rows(u):
        place = core * 2 + pair_of(t)[0]
        return w_hbm.at[pl.ds((u * 4 + place) * wall.shape[3], wall.shape[3])]

    def wz_copy(u, sender):
        return pltpu.make_async_remote_copy(
            src_ref=own_rows(u), dst_ref=wall.at[sender, core, pair_of(sender)[0]],
            send_sem=wz_send.at[u], recv_sem=wz_recv.at[sender],
            device_id=(me, u), device_id_type=MESH,
        )

    def wp_copy(u):
        b, partner = pair_of(u)
        piece = wall.at[u, core, b]
        return pltpu.make_async_remote_copy(
            src_ref=piece, dst_ref=piece, send_sem=wp_send.at[u], recv_sem=wp_recv.at[u],
            device_id=(partner, t), device_id_type=MESH,
        )

    def ws_copy(u, k):
        b = pair_of(u)[0]
        piece = wall.at[u, core, (b + k) % 2]
        return pltpu.make_async_remote_copy(
            src_ref=piece, dst_ref=piece, send_sem=ws_send.at[u, k], recv_sem=ws_recv.at[u, k],
            device_id=(y * 8 + x * 2 + 1 - core, t), device_id_type=MESH,
        )

    own_weight = pltpu.make_async_copy(
        own_rows(t), wall.at[t, core, pair_of(t)[0]], own_sem.at[0]
    )

    def weight_z(*hops):
        for d in hops:
            wz_copy((t + d) % TZ, t).start()

    steps = ((4,), (3, 5), (2, 6), (1, 7), (0,))

    def weight_first(s):
        for d in steps[s]:
            u = (t + d) % TZ
            if d:
                wz_copy(t, u).wait_recv()
            else:
                own_weight.wait()
            wp_copy(u).start()
            ws_copy(u, 0).start()

    def weight_second(s):
        for d in steps[s]:
            u = (t + d) % TZ
            wp_copy(u).wait_recv()
            ws_copy(u, 1).start()

    def weight_third(s):
        for d in steps[s]:
            u = (t + d) % TZ
            ws_copy(u, 0).wait_recv()
            ws_copy(u, 1).wait_recv()

    tall = 256
    segs_of_tile = tall // x_ref.shape[1]
    tiles = x_ref.shape[0] // segs_of_tile

    def right_copy(s, i):
        at = pl.ds(i * tall, tall)
        return pltpu.make_async_remote_copy(
            src_ref=right_out.at[s, at], dst_ref=right_in.at[s, at],
            send_sem=right_send.at[s, i], recv_sem=right_recv.at[s, i],
            device_id=(me, (t + 1) % TZ), device_id_type=MESH,
        )

    def left_copy(s, i):
        at = pl.ds(i * tall, tall)
        return pltpu.make_async_remote_copy(
            src_ref=left_out.at[s, at], dst_ref=left_in.at[s, at],
            send_sem=left_send.at[s, i], recv_sem=left_recv.at[s, i],
            device_id=(me, (t + TZ - 1) % TZ), device_id_type=MESH,
        )

    def weight_of(share, k):
        wide_rows = wall[share].reshape((x_ref.shape[2],) + wall.shape[4:])
        wnow[k] = wide_rows.reshape(wnow.shape[1:])

    def base_part(k, i):
        rows = x_ref[pl.ds(i * segs_of_tile, segs_of_tile)].reshape(tall, x_ref.shape[2])
        return jnp.dot(rows, wnow[k], preferred_element_type=jnp.float32)

    def pass_right(s, i, value):
        at = pl.ds(i * tall, tall)
        if s > i:
            right_copy(s - 1, i).wait_recv()
            value = value + right_in[s - 1, at].astype(jnp.float32)
        right_out[s, at] = value.astype(jnp.bfloat16)
        right_copy(s, i).start()

    def pass_left(s, i, value):
        at = pl.ds(i * tall, tall)
        if s > 1 - i:
            left_copy(s - 1, i).wait_recv()
            value = value + left_in[s - 1, at].astype(jnp.float32)
        left_out[s, at] = value.astype(jnp.bfloat16)
        left_copy(s, i).start()

    def ring(s):
        for k, d in enumerate(steps[s]):
            weight_of((t + d) % TZ, k)
        if s == 0:
            pass_right(0, 0, base_part(0, 0))
            pass_left(0, 1, base_part(0, 1))
        else:
            for i in range(tiles):
                pass_right(s, i, base_part(0, i))
                pass_left(s, i, base_part(1, i))

    def ring_end():
        weight_of(t, 0)
        for i in range(tiles):
            at = pl.ds(i * tall, tall)
            value = base_part(0, i)
            left_copy(3, i).wait_recv()
            right_copy(3, i).wait_recv()
            value = value + right_in[3, at].astype(jnp.float32) + left_in[3, at].astype(jnp.float32)
            base_ref[pl.ds(i * segs_of_tile, segs_of_tile)] = value.reshape(
                segs_of_tile, base_ref.shape[1], base_ref.shape[2]
            )

    per_seg = x_raw.shape[0] // x_ref.shape[0]

    def by_rows(raw, ref):
        def one(s, _):
            ref[s] = raw[pl.ds(s * per_seg, per_seg)].reshape(ref.shape[1:])
            return 0

        lax.fori_loop(0, ref.shape[0], one, 0)

    loads[0].wait()
    by_rows(x_raw, x_ref)
    for chunk in range(CHUNKS):
        def fill(j, _, chunk=chunk):
            group = moved(me, offset(chunk, j), 1)
            xs[chunk * PER + j] = x_ref[seg_of_group[group]]
            return 0

        lax.fori_loop(0, PER, fill, 0)
    pl.semaphore_wait(barrier, SLOTS - 1 + TZ - 1)
    own_weight.start()

    def send_inputs(chunk):
        def send(j, _):
            x_copy(chunk, j).start()
            return 0

        lax.fori_loop(1 if chunk == 0 else 0, PER, send, 0)

    def packed_shrink(shrink):
        mid = shrink.shape[0] // 2
        value = jnp.concatenate([shrink[:mid, 128:], shrink[mid:, 128:]], axis=1)
        return jnp.concatenate([shrink[:, :128], value], axis=0)

    def shrink_parts(chunk):
        def one(j, _):
            p = chunk * PER + j
            rows = xs[0] if chunk == 0 and isinstance(j, int) else xr[p]
            w = down_ref[local_of_replica[moved(me, offset(chunk, j), -1)]]
            shrink = lax.dot_general(
                rows, w, (((1,), (1,)), ((), ())), preferred_element_type=jnp.float32
            )
            part[p] = packed_shrink(shrink).astype(jnp.bfloat16)
            return 0

        def arrived(j, _):
            x_copy(chunk, j).wait_recv()
            return one(j, 0)

        if chunk == 0:
            one(0, 0)
        lax.fori_loop(1 if chunk == 0 else 0, PER, arrived, 0)

        def send(i, _):
            rs_copy(chunk, (t + i) % TZ, t).start()
            return 0

        lax.fori_loop(1, TZ, send, 0)

    def add_up(chunk):
        def wait(i, _):
            rs_copy(chunk, t, (t + TZ - i) % TZ).wait_recv()
            return 0

        lax.fori_loop(1, TZ, wait, 0)
        rs[chunk, t] = part[chunk * PER + t]
        total = rs[chunk, 0].astype(jnp.float32)
        for u in range(1, TZ):
            total = total + rs[chunk, u].astype(jnp.float32)
        ag[chunk, t] = total.astype(jnp.bfloat16)

        def send(i, _):
            ag_copy(chunk, (t + i) % TZ, t).start()
            return 0

        lax.fori_loop(1, TZ, send, 0)

    def give_back(chunk):
        def wait(i, _):
            ag_copy(chunk, t, (t + TZ - i) % TZ).wait_recv()
            return 0

        lax.fori_loop(1, TZ, wait, 0)

        def deltas(j):
            a = local_of_replica[moved(me, offset(chunk, j), -1)]
            both = ag[chunk, j]
            mid = both.shape[0] // 3
            shrink, value = both[: 2 * mid], both[2 * mid :]
            value = jnp.concatenate([value[:, :64], value[:, 64:]], axis=0)
            q = jnp.dot(shrink[:, 0:64], upq_ref[a], preferred_element_type=jnp.float32)
            k = jnp.dot(shrink[:, 64:128], upkv_ref[a, 0], preferred_element_type=jnp.float32)
            v = jnp.dot(value, upkv_ref[a, 1], preferred_element_type=jnp.float32)
            return jnp.concatenate([q, k, v], axis=1).astype(jnp.bfloat16)

        def one(j, _):
            ds[chunk * PER + j] = deltas(j)
            d_copy(chunk, j).start()
            return 0

        if chunk == 0:
            dr[me] = deltas(0)
        lax.fori_loop(1 if chunk == 0 else 0, PER, one, 0)

    half = 8
    heads = q_ref.shape[2] // HEAD_WIDTH
    wide = q_ref.shape[2]
    rows = half * 2
    n = heads * rows
    unit = math.log2(math.e) / math.sqrt(HEAD_WIDTH)

    old_keys = half * CTX
    all_keys = same.shape[1]

    def prepare():
        row = lax.broadcasted_iota(jnp.int32, same.shape, 0) % rows
        col = lax.broadcasted_iota(jnp.int32, same.shape, 1)
        new = col - old_keys
        old_fits = jnp.where(row // 2 == col // CTX, 0.0, -jnp.inf)
        new_fits = jnp.where((row // 2 == new // 2) & (new <= row), 0.0, -jnp.inf)
        same[...] = jnp.where(new < 0, old_fits, new_fits)
        loads[5].wait()
        by_rows(q_raw, q_ref)

    def attend():
        spot = lax.broadcasted_iota(jnp.int32, (1, old_keys), 1)
        owner, nth = spot // CTX, spot % CTX
        pad = jnp.zeros((all_keys - old_keys - rows, HEAD_WIDTH), jnp.bfloat16)
        ones = jnp.ones((all_keys, HEAD_WIDTH), jnp.bfloat16)
        no_bias = jnp.zeros((1, all_keys - old_keys), jnp.float32)

        def segment(seg):
            delta = dr[group_of_seg[seg]].astype(jnp.float32) * ADAPTER_SCALE
            q_all = (q_ref[seg].astype(jnp.float32) + delta[:, :wide]).astype(jnp.bfloat16)
            fresh = (base_ref[seg] + delta[:, wide:]).astype(jnp.bfloat16)
            outs = []
            for h in range(2):
                at = slice(h * rows, (h + 1) * rows)
                q = jnp.concatenate(
                    [q_all[at, g * HEAD_WIDTH : (g + 1) * HEAD_WIDTH] for g in range(heads)], axis=0
                )
                keys = cache_ref[seg, h * half : (h + 1) * half, 0].reshape(old_keys, HEAD_WIDTH)
                values = cache_ref[seg, h * half : (h + 1) * half, 1].reshape(old_keys, HEAD_WIDTH)
                keys = jnp.concatenate([keys, fresh[at, :HEAD_WIDTH], pad], axis=0)
                values = jnp.concatenate([values, fresh[at, HEAD_WIDTH:], pad], axis=0)
                values = jnp.concatenate([values, ones], axis=1)
                ends = jnp.zeros(spot.shape, jnp.int32)
                for i in range(half):
                    ends = jnp.where(owner == i, lengths[seg * 2 * half + h * half + i], ends)
                bias = jnp.concatenate([jnp.where(nth < ends, 0.0, -jnp.inf), no_bias], axis=1)
                scores = lax.dot_general(
                    q, keys, (((1,), (1,)), ((), ())), preferred_element_type=jnp.float32
                )
                scores = scores + (same[...] + bias)
                lifted = jnp.exp2((scores - jnp.max(scores, axis=1, keepdims=True)) * unit)
                mixed = jnp.dot(lifted.astype(jnp.bfloat16), values, preferred_element_type=jnp.float32)
                mixed = mixed[:, :HEAD_WIDTH] / mixed[:, HEAD_WIDTH:]
                out = jnp.concatenate(
                    [mixed[g * rows : (g + 1) * rows] for g in range(heads)], axis=1
                )
                place = h * half + lax.broadcasted_iota(jnp.int32, out.shape, 0) // 2
                outs.append(jnp.where(place < live[seg], out, 0.0).astype(jnp.bfloat16))
            return jnp.concatenate(outs, axis=0).reshape((per_seg,) + out_ref.shape[1:])

        def four(i, _):
            outs = [segment(4 * i + k) for k in range(4)]
            for k in range(4):
                out_ref[pl.ds((4 * i + k) * per_seg, per_seg)] = outs[k]
            return 0

        lax.fori_loop(0, x_ref.shape[0] // 4, four, 0)

    def returned(chunk):
        def wait(j, _):
            d_copy(chunk, j).wait_recv()
            return 0

        lax.fori_loop(1 if chunk == 0 else 0, PER, wait, 0)

    weight_z(4, 3, 5)
    send_inputs(0)
    send_inputs(1)
    prepare()
    loads[1].wait()
    shrink_parts(0)
    weight_z(2, 6, 1, 7)
    weight_first(0)
    send_inputs(2)
    send_inputs(3)
    loads[2].wait()
    loads[3].wait()
    weight_second(0)
    weight_first(1)
    add_up(0)
    weight_third(0)
    ring(0)
    shrink_parts(1)
    weight_second(1)
    weight_first(2)
    give_back(0)
    weight_third(1)
    ring(1)
    add_up(1)
    shrink_parts(2)
    weight_second(2)
    weight_first(3)
    weight_first(4)
    shrink_parts(3)
    add_up(2)
    give_back(1)
    weight_third(2)
    ring(2)
    weight_second(3)
    weight_second(4)
    add_up(3)
    give_back(2)
    weight_third(3)
    ring(3)
    give_back(3)
    weight_third(4)
    ring_end()
    loads[4].wait()
    for chunk in range(CHUNKS):
        returned(chunk)
    attend()

    for chunk in range(CHUNKS):
        def settle(j, _, chunk=chunk):
            x_copy(chunk, j).wait_send()
            d_copy(chunk, j).wait_send()
            return 0

        lax.fori_loop(1 if chunk == 0 else 0, PER, settle, 0)

        def settle_z(i, _, chunk=chunk):
            rs_copy(chunk, (t + i) % TZ, t).wait_send()
            ag_copy(chunk, (t + i) % TZ, t).wait_send()
            return 0

        lax.fori_loop(1, TZ, settle_z, 0)

    def settle_w(i, _):
        wz_copy((t + i) % TZ, t).wait_send()
        return 0

    lax.fori_loop(1, TZ, settle_w, 0)
    def settle_shares(u, _):
        wp_copy(u).wait_send()
        ws_copy(u, 0).wait_send()
        ws_copy(u, 1).wait_send()
        return 0

    lax.fori_loop(0, TZ, settle_shares, 0)

    for s in range(4):
        for i in range(tiles):
            if s >= i:
                right_copy(s, i).wait_send()
            if s >= 1 - i:
                left_copy(s, i).wait_send()


def layer(tables, x, down, upq, upkv, q, cache, weight):
    segs = tables[1].shape[0]
    tokens, features = x.shape[1:]
    per_seg = x.shape[0] // segs
    rows = per_seg * tokens
    packed_rows = rows * down.shape[1] // HEAD_WIDTH
    kv = weight.shape[1] * weight.shape[2]
    wide = q.shape[2]
    columns = wide + kv
    smem = pl.BlockSpec(memory_space=pltpu.SMEM)
    vmem = pl.BlockSpec(memory_space=pltpu.VMEM)
    hbm = pl.BlockSpec(memory_space=pltpu.HBM)
    dma = pltpu.SemaphoreType.DMA
    tiles = segs * rows // 256
    half_rows = rows // 2 * (wide // HEAD_WIDTH)
    loaded = [x, down, upq, upkv, q, cache]

    def room(*shape, dtype=jnp.bfloat16):
        return pltpu.VMEM(shape, dtype)

    return pl.pallas_call(
        layer_kernel,
        out_shape=jax.ShapeDtypeStruct(q.shape, jnp.bfloat16),
        in_specs=[smem] * len(tables) + [hbm] * (len(loaded) + 1),
        out_specs=vmem,
        scratch_shapes=[room(*a.shape) for a in loaded]
        + [
            dma((len(loaded),)),
            room(segs, rows, features),
            room(segs, rows, wide),
            room(segs, rows, kv, dtype=jnp.float32),
            room(half_rows, rows // 4 * CTX + 128, dtype=jnp.float32),
            room(SLOTS, rows, features),
            room(SLOTS, rows, features),
            room(SLOTS, packed_rows, HEAD_WIDTH),
            room(CHUNKS, TZ, packed_rows, HEAD_WIDTH),
            room(CHUNKS, TZ, packed_rows, HEAD_WIDTH),
            room(SLOTS, rows, columns),
            room(SLOTS, rows, columns),
            room(TZ, 2, 2, features // 4, *weight.shape[1:]),
            room(4, segs * rows, kv),
            room(4, segs * rows, kv),
            room(4, segs * rows, kv),
            room(4, segs * rows, kv),
            room(2, features, kv),
            dma((SLOTS,)), dma((SLOTS,)),
            dma((CHUNKS, TZ)), dma((CHUNKS, TZ)), dma((CHUNKS, TZ)), dma((CHUNKS, TZ)),
            dma((SLOTS,)), dma((SLOTS,)),
            dma((TZ,)), dma((TZ,)),
            dma((TZ,)), dma((TZ,)), dma((TZ, 2)), dma((TZ, 2)), dma((1,)),
            dma((4, tiles)), dma((4, tiles)), dma((4, tiles)), dma((4, tiles)),
        ],
        compiler_params=pltpu.CompilerParams(
            collective_id=0, has_side_effects=True, vmem_limit_bytes=52 * 2**20
        ),
        name="layer",
    )(*tables, *loaded, weight)


def shards(
    normed_token_input,
    rotated_base_query,
    key_value_weight,
    key_value_cache,
    adapter_down_maps,
    query_up_maps,
    key_value_up_maps,
    adapter_storage_row,
    segment_adapter,
    segment_live_requests,
    cache_length,
):
    requests, tokens, features = normed_token_input.shape
    wide = rotated_base_query.shape[2]
    kv_wide = key_value_weight.shape[2]
    owned = adapter_down_maps.shape[0]
    replicas = lax.axis_size("replica")
    segs = segment_live_requests.shape[0]
    me = lax.axis_index("replica")

    adapter_ids = jnp.arange(adapter_storage_row.shape[0], dtype=jnp.int32)
    slot = jnp.sum(
        jnp.where(
            segment_adapter[:, None] == adapter_ids[None, :], adapter_storage_row[None, :], 0
        ),
        axis=1,
    ).reshape(replicas, segs)
    group, local = lax.div(slot, owned), lax.rem(slot, owned)
    group_of_seg = lax.dynamic_index_in_dim(group, me, 0, keepdims=False)
    group_ids = jnp.arange(replicas, dtype=jnp.int32)
    seg_ids = jnp.arange(segs, dtype=jnp.int32)
    seg_of_group = jnp.sum(
        jnp.where(group_of_seg[None, :] == group_ids[:, None], seg_ids[None, :], 0), axis=1
    )
    local_of_replica = jnp.sum(jnp.where(group == me, local, 0), axis=1)

    return layer(
        (seg_of_group, group_of_seg, local_of_replica, segment_live_requests, cache_length),
        normed_token_input, adapter_down_maps, query_up_maps, key_value_up_maps,
        rotated_base_query,
        key_value_cache.reshape((segs, requests // segs) + key_value_cache.shape[1:]),
        key_value_weight,
    )


def solution(mesh):
    return jax.shard_map(
        shards,
        mesh=mesh,
        in_specs=(
            P("replica", None, "tensor"),
            P("replica", None, "tensor"),
            P(None, None, "tensor"),
            P("replica", None, None, "tensor"),
            P("replica", None, "tensor"),
            P("replica", None, "tensor"),
            P("replica", None, None, "tensor"),
            P(),
            P(),
            P("replica"),
            P("replica"),
        ),
        out_specs=P("replica", None, "tensor"),
        check_vma=False,
    )
```
